256 devices in a mesh: tm: 2 (over core), row: 4 (over x), col: 32 (over z, y).
Axes of the slice: x: 4, y: 4, z: 8, core: 2. Of those that a mesh axis runs over, the one named last changes fastest.
Arguments:
- latent: bfloat16 [8, 136, 256, 256], P('tm', 'row', 'col'), may hold values from -6 to 6
- conv_cache: bfloat16 [3, 2, 136, 256, 256], P(None, None, 'row', 'col'), may hold values from -6 to 6
- conv_weight: bfloat16 [3, 3, 3, 3, 256, 256], replicated, may hold values from -0.078125 to 0.078125
- conv_bias: float32 [3, 256], replicated, may hold values from -3 to 3
- w_query: bfloat16 [256, 256], replicated, may hold values from -16 to 16
- w_key: bfloat16 [256, 256], replicated, may hold values from -0.375 to 0.375
- w_value: bfloat16 [256, 256], replicated, may hold values from -0.375 to 0.375
- w_out: bfloat16 [256, 256], replicated, may hold values from -0.375 to 0.375
- cache_key: bfloat16 [2, 136, 256, 256], P(None, 'row', 'col'), may hold values from -6 to 6
- cache_value: bfloat16 [2, 136, 256, 256], P(None, 'row', 'col'), may hold values from -6 to 6
Outputs:
- encoded: bfloat16 [8, 136, 256, 256], P('tm', 'row', 'col')
The draws below stay inside these ranges and needn't reach their ends.
All inputs are finite; a program needn't handle non-finite values.
Results may differ from the reference program's by a relative error of at most 0.04.
Values may be sent and summed in bfloat16 or wider, within the bound.
No kernel may reach another device: no remote copies, remote signals or barrier semaphores. Data moves between devices by JAX's collectives and lax.ppermute only.
A program may use at most 128 MiB of HBM per device.

```python
import jax
import jax.numpy as jnp
from jax import lax

C = 256
HEADS = 8
HD = 32
LAYERS = 3
BLOCK = 2
HEIGHT = 136
WIDTH = 256
FRAMES = 8


def draw_w_query(key, part):
    base = jnp.clip(jax.random.normal(key, (C, C), jnp.float32), -6.0, 6.0) * C ** (-0.5)
    return base.astype(jnp.bfloat16)


def levels(key, extent, pieces, smallest, high):
    loudness, own = 1.0, jax.random.fold_in(key, 6)
    for dim, parts in pieces:
        heights = jnp.exp(jax.random.uniform(jax.random.fold_in(own, dim), (parts,), jnp.float32, smallest / len(pieces), high / len(pieces)))
        loudness = loudness * jnp.repeat(heights, extent[dim] // parts).reshape([-1 if axis == dim else 1 for axis in range(len(extent))])
    return loudness


def normal_values(rng, shape, deviation, most, pieces=(), kind=jnp.bfloat16):
    array = jax.random.normal(rng, shape, jnp.float32) * deviation
    if len(pieces) > 0:
        array = levels(rng, shape, pieces, -0.22, 0.18) * array
    return jnp.clip(array, min=-most, max=most).astype(kind)


def setup_inputs(seed: int = 0) -> dict:
    key_list = jax.random.split(jax.random.key(seed), 11)
    latent = normal_values(key_list[0], (FRAMES, HEIGHT, WIDTH, C), 1.0, 6.0, ((0, 2), (1, 4), (2, 32)))
    conv_cache = normal_values(key_list[1], (LAYERS, 2, HEIGHT, WIDTH, C), 1.0, 6.0, ((2, 4), (3, 32)))
    conv_weight = normal_values(key_list[2], (LAYERS, 3, 3, 3, C, C), (27 * C) ** -0.5, 0.078125)
    conv_bias = normal_values(key_list[3], (LAYERS, C), 0.5, 3.0, (), jnp.float32)
    w_query = draw_w_query(jax.random.fold_in(key_list[10], 71), 0)
    w_key = normal_values(key_list[5], (C, C), C ** -0.5, 0.375)
    w_value = normal_values(key_list[6], (C, C), C ** -0.5, 0.375)
    w_out = normal_values(key_list[7], (C, C), C ** -0.5, 0.375)
    cache_key = normal_values(key_list[8], (BLOCK, HEIGHT, WIDTH, C), 1.0, 6.0, ((1, 4), (2, 32)))
    cache_value = normal_values(key_list[9], (BLOCK, HEIGHT, WIDTH, C), 1.0, 6.0, ((1, 4), (2, 32)))
    return dict(latent=latent, conv_cache=conv_cache, conv_weight=conv_weight, conv_bias=conv_bias, w_query=w_query, w_key=w_key, w_value=w_value, w_out=w_out, cache_key=cache_key, cache_value=cache_value)


def causal_conv(frames, history, kernel, bias):
    extended = jnp.concatenate([history, frames], 0)
    padded = jnp.pad(extended, ((0, 0), (1, 1), (1, 1), (0, 0)))
    count, height, width, chans = frames.shape
    total = jnp.zeros((count * height * width, kernel.shape[-1]), jnp.float32)
    for a in range(3):
        for b in range(3):
            for c in range(3):
                window = padded[a:a + count, b:b + height, c:c + width].reshape(-1, chans)
                total = total + jnp.dot(window, kernel[a, b, c], preferred_element_type=jnp.float32)
    total = total + bias.astype(jnp.float32)[None, :]
    return total.reshape(count, height, width, -1)

def attend(query, keys, values, past_key, past_value):
    frames, pixels, chans = query.shape
    span = past_key.shape[0] + frames
    all_keys = jnp.concatenate([past_key, keys], 0).astype(jnp.float32).reshape(span, pixels, HEADS, HD)
    all_values = jnp.concatenate([past_value, values], 0).astype(jnp.float32).reshape(span, pixels, HEADS, HD)
    q_heads = query.astype(jnp.float32).reshape(frames, pixels, HEADS, HD)
    scores = jnp.einsum('tphd,sphd->tsph', q_heads, all_keys) * HD ** (-0.5)
    query_ids = jnp.arange(frames, dtype=jnp.int32)[:, None]
    key_ids = jnp.arange(span, dtype=jnp.int32)[None, :]
    visible = (key_ids < BLOCK) | ((key_ids - BLOCK) // BLOCK <= query_ids // BLOCK)
    visible = visible[:, :, None, None]
    scores = jnp.where(visible, scores, -1e+30)
    peak = lax.optimization_barrier(jnp.max(scores, axis=1, keepdims=True))
    weights = jnp.where(visible, jnp.exp(scores - peak), 0.0)
    probs = weights / lax.optimization_barrier(jnp.sum(weights, axis=1, keepdims=True))
    mixed = jnp.einsum('tsph,sphd->tphd', probs, all_values)
    return mixed.reshape(frames, pixels, chans).astype(jnp.bfloat16)

def reference(latent, conv_cache, conv_weight, conv_bias, w_query, w_key, w_value, w_out, cache_key, cache_value):
    current = latent
    hidden = latent
    for layer in range(LAYERS):
        value = causal_conv(current, conv_cache[layer], conv_weight[layer], conv_bias[layer])
        if layer < LAYERS - 1:
            current = jax.nn.silu(value).astype(jnp.bfloat16)
        else:
            hidden = (latent.astype(jnp.float32) + value).astype(jnp.bfloat16)
    frames, height, width, chans = hidden.shape
    pixels = height * width
    wide = hidden.astype(jnp.float32).reshape(-1, chans)
    normed = (wide * lax.rsqrt(lax.optimization_barrier(jnp.mean(wide * wide, -1, keepdims=True)) + 1e-06)).astype(jnp.bfloat16)
    query = jnp.dot(normed, w_query, preferred_element_type=jnp.float32).astype(jnp.bfloat16).reshape(frames, pixels, chans)
    keys = jnp.dot(normed, w_key, preferred_element_type=jnp.float32).astype(jnp.bfloat16).reshape(frames, pixels, chans)
    values = jnp.dot(normed, w_value, preferred_element_type=jnp.float32).astype(jnp.bfloat16).reshape(frames, pixels, chans)
    mixed = attend(query, keys, values, cache_key.reshape(BLOCK, pixels, chans), cache_value.reshape(BLOCK, pixels, chans))
    projected = jnp.dot(mixed.reshape(-1, chans), w_out, preferred_element_type=jnp.float32)
    return (wide + projected).astype(jnp.bfloat16).reshape(frames, height, width, chans)
```

```python
import functools

import jax
import jax.numpy as jnp
from jax import lax
from jax.experimental import pallas as pl
from jax.experimental.pallas import tpu as pltpu
from jax.sharding import PartitionSpec as P

HEADS = 8
HD = 32
C = 256
T = 8
FRAMES = 4
ROWS = 34
HALF = 17
COLS = 8
EXT = HALF + 6
BF = jnp.bfloat16
F32 = jnp.float32
TAPS = [(a, b, c) for a in range(3) for b in range(3) for c in range(3)]
LAYER_K = 27 * C

ANY = pl.BlockSpec(memory_space=pl.ANY)
VM = pl.BlockSpec(memory_space=pltpu.VMEM)


def shape(*dims, dtype=BF):
    return jax.ShapeDtypeStruct(dims, dtype)


def run_copies(copies):
    for copy in copies:
        copy.start()
    for copy in copies:
        copy.wait()


def pack_rows(latent, cache, out_a, out_b, sems):
    half = lax.axis_index("tm")
    row_a = 31 * (1 - half)
    row_b = 31 * half
    run_copies([
        pltpu.make_async_copy(latent.at[:, pl.ds(row_a, 3)], out_a.at[0:4], sems.at[0]),
        pltpu.make_async_copy(cache.at[:, pl.ds(row_a, 3)], out_a.at[4:10], sems.at[1]),
        pltpu.make_async_copy(latent.at[:, pl.ds(row_b, 3)], out_b, sems.at[2]),
    ])


def assemble(own, other, cache, halo_a, halo_b, lt, ht, left, right, stage, wide, sems):
    half = lax.axis_index("tm")
    first, second = 4 * half, 4 - 4 * half
    start, at, edge = 14 * half, 3 - 3 * half, 20 * half
    run_copies([
        pltpu.make_async_copy(
            own.at[:, pl.ds(start, 20)], stage.at[pl.ds(first, 4), pl.ds(at, 20)], sems.at[0]),
        pltpu.make_async_copy(
            other.at[:, pl.ds(start, 20)], stage.at[pl.ds(second, 4), pl.ds(at, 20)], sems.at[1]),
        pltpu.make_async_copy(
            cache.at[:, pl.ds(start, 20)], stage.at[8:14, pl.ds(at, 20)], sems.at[2]),
        pltpu.make_async_copy(
            halo_a.at[0:4], stage.at[pl.ds(first, 4), pl.ds(edge, 3)], sems.at[3]),
        pltpu.make_async_copy(halo_a.at[4:10], stage.at[8:14, pl.ds(edge, 3)], sems.at[4]),
        pltpu.make_async_copy(
            halo_b, stage.at[pl.ds(second, 4), pl.ds(edge, 3)], sems.at[5]),
    ])
    sub = lax.broadcasted_iota(jnp.int32, (T, C), 0)
    for slot in range(4):
        wide[slot, 14 * COLS:16 * COLS] = jnp.zeros((2 * COLS, 128), F32)

    def row(e, slot):
        for frame in range(14):
            v = stage[frame, e].astype(F32)
            wide[2 * slot, frame * COLS:(frame + 1) * COLS] = v[:, :128]
            wide[2 * slot + 1, frame * COLS:(frame + 1) * COLS] = v[:, 128:]
        past = []
        for col in range(COLS):
            lat = jnp.concatenate(
                [wide[2 * slot + lane, pl.ds(col, T, stride=COLS)] for lane in (0, 1)], 1)
            old = jnp.concatenate(
                [wide[2 * slot + lane, pl.ds(T * COLS + col, T, stride=COLS)]
                 for lane in (0, 1)], 1)
            lt[e, col] = lat.astype(BF)
            ht[e, col] = old.astype(BF)
            past.append(old)
            if col < 3:
                left[e, col] = lat.astype(BF)
            if col >= 5:
                right[e, col - 5] = lat.astype(BF)
        left[e, 3] = jnp.where(sub < 6, past[0], pltpu.roll(past[2], 6, 0)).astype(BF)
        left[e, 4] = past[1].astype(BF)
        right[e, 3] = jnp.where(sub < 6, past[7], pltpu.roll(past[5], 6, 0)).astype(BF)
        right[e, 4] = past[6].astype(BF)

    def pair(i, carry):
        row(2 * i, 0)
        row(2 * i + 1, 1)
        return carry

    lax.fori_loop(0, EXT // 2, pair, 0)
    row(EXT - 1, 0)


def put(dst, r, at, now, past, layer):
    n = now.shape[0]
    sub = lax.broadcasted_iota(jnp.int32, (n, T, C), 1)

    def roll(v, k):
        k %= T
        return v if k == 0 else pltpu.roll(v, k, 1)

    dst[2, r, at:at + n] = now
    dst[1, r, at:at + n] = jnp.where(sub < 1, roll(past, -2 * layer - 1), roll(now, 1))
    dst[0, r, at:at + n] = jnp.where(sub < 2, roll(past, -2 * layer), roll(now, 2))


def conv(src, rows, groups, weights, bias):
    total = None
    count = sum(n for _, n in groups)
    for a in range(3):
        for b in range(3):
            parts = []
            for c in range(3):
                cols = [src[a, b:b + rows, first + c:first + c + n] for first, n in groups]
                block = cols[0] if len(cols) == 1 else jnp.concatenate(cols, 1)
                parts.append(block.reshape(rows * count * T, C).astype(BF))
            k = (a * 3 + b) * 3 * C
            part = jnp.dot(
                jnp.concatenate(parts, 1), weights[k:k + 3 * C], preferred_element_type=F32)
            total = part if total is None else total + part
    return (total + bias).reshape(rows, count, T, C)


def silu(v):
    return v / (1.0 + jnp.exp(-v))


def row_limits(border):
    half, place = lax.axis_index("tm"), lax.axis_index("row")
    low = jnp.where((half == 0) & (place == 0), border, 0)
    high = jnp.where(
        (half == 1) & (place == lax.axis_size("row") - 1), HALF + border, HALF + 2 * border)
    return low, high


def weight_copies(weights, held, sems):
    third = LAYER_K // 3
    return [
        pltpu.make_async_copy(
            weights.at[pl.ds(i * third, third)], held.at[pl.ds(i * third, third)], sems.at[i])
        for i in range(9)
    ]


def interior(lt, ht, weights, bias, out1, out2, out3, x, y, z, res, held, sems):
    copies = weight_copies(weights, held, sems)
    for copy in copies:
        copy.start()

    def fill(r, carry):
        put(x, r, 0, lt[r].astype(F32), ht[r].astype(F32), 0)
        return carry

    lax.fori_loop(0, EXT, fill, 0)
    for copy in copies[0:3]:
        copy.wait()
    res[...] = conv(x, 21, [(0, 6)], held[0:LAYER_K], bias[0:1])
    low, high = row_limits(2)

    def one(r, carry):
        v = jnp.where((r >= low) & (r < high), silu(res[r]), 0.0).astype(BF)
        out1[r, 0:2] = v[0:2]
        out1[r, 2:4] = v[4:6]
        put(y, r, 0, v.astype(F32), ht[r + 1, 1:7].astype(F32), 1)
        return carry

    lax.fori_loop(0, 21, one, 0)
    for copy in copies[3:6]:
        copy.wait()
    res[0:19, 0:4] = conv(y, 19, [(0, 4)], held[LAYER_K:2 * LAYER_K], bias[1:2])
    low2, high2 = row_limits(1)

    def two(r, carry):
        v = jnp.where((r >= low2) & (r < high2), silu(res[r, 0:4]), 0.0).astype(BF)
        out2[r] = v
        put(z, r, 0, v.astype(F32), ht[r + 2, 2:6].astype(F32), 2)
        return carry

    lax.fori_loop(0, 19, two, 0)
    for copy in copies[6:9]:
        copy.wait()
    last = conv(z, 17, [(0, 2)], held[2 * LAYER_K:3 * LAYER_K], bias[2:3])
    out3[...] = (last + lt[3:20, 3:5].astype(F32)).astype(BF)


def exterior(lt, ht, from_left, from_right, in1, in2, in3, weights, bias, wq, wk, wv, wo,
             key_cache, value_cache, mine, theirs, x, y, z, res, held, hid, qs, ks, vs, mix,
             ck, cv, ckw, cvw, enc, sems):
    half = lax.axis_index("tm")
    copies = weight_copies(weights, held, sems)
    for copy in copies:
        copy.start()
    more = [
        pltpu.make_async_copy(key_cache.at[:, pl.ds(HALF * half, HALF)], ck, sems.at[9]),
        pltpu.make_async_copy(value_cache.at[:, pl.ds(HALF * half, HALF)], cv, sems.at[10]),
    ]
    for copy in more:
        copy.start()
    place = lax.axis_index("col")
    has_left = place > 0
    has_right = place < lax.axis_size("col") - 1
    groups = [(0, 3), (5, 3)]

    def fill(r, carry):
        for side, at, own in ((from_left, 0, 3), (from_right, 7, 5)):
            t1 = side[r, 3].astype(F32)
            t2 = side[r, 4].astype(F32)
            t3 = pltpu.roll(t1, 2, 0)
            order = (t3, t2, t1) if at == 0 else (t1, t2, t3)
            past = jnp.concatenate([v[None] for v in order], 0)
            put(x, r, at, side[r, 0:3].astype(F32), past, 0)
        put(x, r, 3, lt[r, 0:2].astype(F32), ht[r, 0:2].astype(F32), 0)
        put(x, r, 5, lt[r, 6:8].astype(F32), ht[r, 6:8].astype(F32), 0)
        return carry

    lax.fori_loop(0, EXT, fill, 0)
    for copy in copies[0:3]:
        copy.wait()
    res[...] = conv(x, 21, groups, held[0:LAYER_K], bias[0:1])
    low, high = row_limits(2)

    def one(r, carry):
        ok = (r >= low) & (r < high)
        v = silu(res[r]).astype(BF).astype(F32)
        zero = jnp.zeros((1, T, C), F32)
        l = [jnp.where(ok & has_left, v[0:2], 0.0), jnp.where(ok, v[2:3], zero)]
        g = [jnp.where(ok, v[3:4], zero), jnp.where(ok & has_right, v[4:6], 0.0)]
        e = r + 1
        put(y, r, 0, jnp.concatenate(l + [in1[r, 0:2].astype(F32)], 0), jnp.concatenate(
            [from_left[e, 4:5].astype(F32), from_left[e, 3:4].astype(F32),
             ht[e, 0:3].astype(F32)], 0), 1)
        put(y, r, 5, jnp.concatenate([in1[r, 2:4].astype(F32)] + g, 0), jnp.concatenate(
            [ht[e, 5:8].astype(F32), from_right[e, 3:4].astype(F32),
             from_right[e, 4:5].astype(F32)], 0), 1)
        return carry

    lax.fori_loop(0, 21, one, 0)
    for copy in copies[3:6]:
        copy.wait()
    res[0:19] = conv(y, 19, groups, held[LAYER_K:2 * LAYER_K], bias[1:2])
    low2, high2 = row_limits(1)

    def two(r, carry):
        ok = (r >= low2) & (r < high2)
        v = silu(res[r]).astype(BF).astype(F32)
        l = [jnp.where(ok & has_left, v[0:1], 0.0), jnp.where(ok, v[1:3], 0.0)]
        g = [jnp.where(ok, v[3:5], 0.0), jnp.where(ok & has_right, v[5:6], 0.0)]
        e = r + 2
        put(z, r, 0, jnp.concatenate(l + [in2[r, 0:2].astype(F32)], 0), jnp.concatenate(
            [from_left[e, 3:4].astype(F32), ht[e, 0:4].astype(F32)], 0), 2)
        put(z, r, 5, jnp.concatenate([in2[r, 2:4].astype(F32)] + g, 0), jnp.concatenate(
            [ht[e, 4:8].astype(F32), from_right[e, 3:4].astype(F32)], 0), 2)
        return carry

    lax.fori_loop(0, 19, two, 0)
    for copy in copies[6:9]:
        copy.wait()
    last = conv(z, 17, groups, held[2 * LAYER_K:3 * LAYER_K], bias[2:3])
    hid[:, 0:3] = (last[:, 0:3] + lt[3:20, 0:3].astype(F32)).astype(BF).astype(F32)
    hid[:, 3:5] = in3[...].astype(F32)
    hid[:, 5:8] = (last[:, 3:6] + lt[3:20, 5:8].astype(F32)).astype(BF).astype(F32)

    wide = hid[...].reshape(HALF * COLS * T, C)
    mean = jnp.mean(wide * wide, -1, keepdims=True)
    normed = (wide * lax.rsqrt(mean + 1e-6)).astype(BF)
    for w, dst in ((wq, qs), (wk, ks), (wv, vs)):
        v = jnp.dot(normed, w[...], preferred_element_type=F32).astype(BF).astype(F32)
        dst[...] = v.reshape(HALF, COLS, T, C)
    for copy in more:
        copy.wait()
    ckw[...] = ck[...].astype(F32)
    cvw[...] = cv[...].astype(F32)
    block = (lax.broadcasted_iota(jnp.int32, (C, C), 0) // HD
             == lax.broadcasted_iota(jnp.int32, (C, C), 1) // HD)
    ones = jnp.where(block, 1.0, 0.0).astype(BF)
    t = lax.broadcasted_iota(jnp.int32, (COLS, T, C), 1)
    scale = HD ** -0.5

    def attend(r, carry):
        q = qs[r] * scale
        k = ks[r]
        v = vs[r]
        products = []
        for f in range(2):
            key = jnp.concatenate(
                [jnp.broadcast_to(ckw[f, r, c:c + 1], (T, C))[None] for c in range(COLS)], 0)
            products.append(q * key)
        for d in range(T):
            products.append(q * (k if d == 0 else pltpu.roll(k, d, 1)))
        flat = jnp.concatenate([p.reshape(COLS * T, C).astype(BF) for p in products], 0)
        sums = jnp.dot(flat, ones, preferred_element_type=F32).reshape(10, COLS, T, C)
        scores = [sums[0], sums[1], sums[2]]
        for d in range(1, T):
            seen = t >= d
            if d == T - 1:
                seen = seen | (t % 2 == 0)
            scores.append(jnp.where(seen, sums[2 + d], -1e30))
        peak = functools.reduce(jnp.maximum, scores)
        weights_ = [jnp.exp(s - peak) for s in scores]
        norm = functools.reduce(jnp.add, weights_)
        acc = weights_[2] * v
        for f in range(2):
            val = jnp.concatenate(
                [jnp.broadcast_to(cvw[f, r, c:c + 1], (T, C))[None] for c in range(COLS)], 0)
            acc = acc + weights_[f] * val
        for d in range(1, T):
            acc = acc + weights_[2 + d] * pltpu.roll(v, d, 1)
        mix[r] = acc / norm
        return carry

    lax.fori_loop(0, HALF, attend, 0)
    mixed = mix[...].reshape(HALF * COLS * T, C).astype(BF)
    done = wide + jnp.dot(mixed, wo[...], preferred_element_type=F32)
    enc[0] = done[:, :128]
    enc[1] = done[:, 128:]

    def turn(r, carry):
        for dst, base in ((mine, 4 * half), (theirs, 4 - 4 * half)):
            for f in range(4):
                v = jnp.concatenate(
                    [enc[lane, pl.ds(r * COLS * T + base + f, COLS, stride=T)]
                     for lane in (0, 1)], 1)
                dst[f, r] = v.astype(BF)
        return carry

    lax.fori_loop(0, HALF, turn, 0)


def local(latent, conv_cache, conv_weight, conv_bias, w_query, w_key, w_value, w_out,
          cache_key, cache_value):
    params = functools.partial(pltpu.CompilerParams)
    cache = conv_cache.reshape(6, ROWS, COLS, C)
    weights = conv_weight.reshape(3 * LAYER_K, C)
    n_row, n_col = lax.axis_size("row"), lax.axis_size("col")

    def device(tm, row):
        return tm * n_row + row

    msg_a, msg_b = pl.pallas_call(
        pack_rows,
        out_shape=(shape(10, 3, COLS, C), shape(4, 3, COLS, C)),
        in_specs=[ANY, ANY],
        out_specs=(ANY, ANY),
        scratch_shapes=[pltpu.SemaphoreType.DMA((3,))],
        name="pack_rows",
    )(latent, cache)
    other = lax.ppermute(latent, "tm", [(0, 1), (1, 0)])
    pairs_a = [(device(0, r), device(0, r + 1)) for r in range(n_row - 1)]
    pairs_a += [(device(1, r + 1), device(1, r)) for r in range(n_row - 1)]
    pairs_b = [(device(1, r), device(0, r + 1)) for r in range(n_row - 1)]
    pairs_b += [(device(0, r + 1), device(1, r)) for r in range(n_row - 1)]
    halo_a = lax.ppermute(msg_a, ("tm", "row"), pairs_a)
    halo_b = lax.ppermute(msg_b, ("tm", "row"), pairs_b)

    tiles = shape(EXT, COLS, T, C)
    side = shape(EXT, 5, T, C)
    lt, ht, left, right = pl.pallas_call(
        assemble,
        out_shape=(tiles, tiles, side, side),
        in_specs=[ANY] * 5,
        out_specs=(VM,) * 4,
        scratch_shapes=[
            pltpu.VMEM((14, EXT, COLS, C), BF),
            pltpu.VMEM((4, 16 * COLS, 128), F32),
            pltpu.SemaphoreType.DMA((6,)),
        ],
        compiler_params=params(vmem_limit_bytes=16 << 20),
        name="assemble",
    )(latent, other, cache, halo_a, halo_b)
    from_right = lax.ppermute(left, "col", [(i + 1, i) for i in range(n_col - 1)])
    from_left = lax.ppermute(right, "col", [(i, i + 1) for i in range(n_col - 1)])

    in1, in2, in3 = pl.pallas_call(
        interior,
        out_shape=(shape(21, 4, T, C), shape(19, 4, T, C), shape(17, 2, T, C)),
        in_specs=[VM, VM, ANY, VM],
        out_specs=(VM,) * 3,
        scratch_shapes=[
            pltpu.VMEM((3, 23, 8, T, C), F32),
            pltpu.VMEM((3, 21, 6, T, C), F32),
            pltpu.VMEM((3, 19, 4, T, C), F32),
            pltpu.VMEM((21, 6, T, C), F32),
            pltpu.VMEM((3 * LAYER_K, C), BF),
            pltpu.SemaphoreType.DMA((9,)),
        ],
        cost_estimate=pl.CostEstimate(
            flops=2 * 1888 * LAYER_K * C, bytes_accessed=14 << 20, transcendentals=0),
        compiler_params=params(vmem_limit_bytes=48 << 20),
        name="interior",
    )(lt, ht, weights, conv_bias)

    pixels = HALF * COLS * T
    mine, theirs = pl.pallas_call(
        exterior,
        out_shape=(shape(4, HALF, COLS, C), shape(4, HALF, COLS, C)),
        in_specs=[VM] * 7 + [ANY] + [VM] * 5 + [ANY] * 2,
        out_specs=(VM, VM),
        scratch_shapes=[
            pltpu.VMEM((3, 23, 10, T, C), F32),
            pltpu.VMEM((3, 21, 10, T, C), F32),
            pltpu.VMEM((3, 19, 10, T, C), F32),
            pltpu.VMEM((21, 6, T, C), F32),
            pltpu.VMEM((3 * LAYER_K, C), BF),
            pltpu.VMEM((HALF, COLS, T, C), F32),
            pltpu.VMEM((HALF, COLS, T, C), F32),
            pltpu.VMEM((HALF, COLS, T, C), F32),
            pltpu.VMEM((HALF, COLS, T, C), F32),
            pltpu.VMEM((HALF, COLS, T, C), F32),
            pltpu.VMEM((2, HALF, COLS, C), BF),
            pltpu.VMEM((2, HALF, COLS, C), BF),
            pltpu.VMEM((2, HALF, COLS, C), F32),
            pltpu.VMEM((2, HALF, COLS, C), F32),
            pltpu.VMEM((2, pixels, 128), F32),
            pltpu.SemaphoreType.DMA((11,)),
        ],
        cost_estimate=pl.CostEstimate(
            flops=2 * 3000 * LAYER_K * C, bytes_accessed=18 << 20, transcendentals=0),
        compiler_params=params(vmem_limit_bytes=56 << 20),
        name="exterior",
    )(lt, ht, from_left, from_right, in1, in2, in3, weights, conv_bias, w_query, w_key, w_value,
      w_out, cache_key, cache_value)
    got = lax.ppermute(theirs, "tm", [(0, 1), (1, 0)])
    top = lax.axis_index("tm") == 0
    return jnp.concatenate([jnp.where(top, mine, got), jnp.where(top, got, mine)], 1)


def solution(mesh):
    return jax.shard_map(
        local,
        mesh=mesh,
        in_specs=(
            P("tm", "row", "col", None),
            P(None, None, "row", "col", None),
            P(),
            P(),
            P(),
            P(),
            P(),
            P(),
            P(None, "row", "col", None),
            P(None, "row", "col", None),
        ),
        out_specs=P("tm", "row", "col", None),
        check_vma=False,
    )
```

```python
import functools

import jax
import jax.numpy as jnp
from jax import lax
from jax.experimental import pallas as pl
from jax.experimental.pallas import tpu as pltpu
from jax.sharding import PartitionSpec as P

HEADS = 8
HD = 32
C = 256
T = 8
FRAMES = 4
ROWS = 34
HALF = 17
COLS = 8
EXT = HALF + 6
BF = jnp.bfloat16
F32 = jnp.float32
TAPS = [(a, b, c) for a in range(3) for b in range(3) for c in range(3)]
LAYER_K = 27 * C

ANY = pl.BlockSpec(memory_space=pl.ANY)
HB = pl.BlockSpec(memory_space=pltpu.HBM)
VM = pl.BlockSpec(memory_space=pltpu.VMEM)


def shape(*dims, dtype=BF):
    return jax.ShapeDtypeStruct(dims, dtype)


def run_copies(copies):
    for copy in copies:
        copy.start()
    for copy in copies:
        copy.wait()


def pack_rows(latent, cache, out_a, out_b, own, old, sems):
    half = lax.axis_index("tm")
    row_a, row_b, start = 31 * (1 - half), 31 * half, 14 * half
    run_copies([
        pltpu.make_async_copy(latent.at[:, pl.ds(row_a, 3)], out_a.at[0:4], sems.at[0]),
        pltpu.make_async_copy(cache.at[:, pl.ds(row_a, 3)], out_a.at[4:10], sems.at[1]),
        pltpu.make_async_copy(latent.at[:, pl.ds(row_b, 3)], out_b, sems.at[2]),
        pltpu.make_async_copy(latent.at[:, pl.ds(start, 20)], own, sems.at[3]),
        pltpu.make_async_copy(cache.at[:, pl.ds(start, 20)], old, sems.at[4]),
    ])


def load_weights(weights, bias, held, held_bias, sems):
    run_copies([
        pltpu.make_async_copy(weights, held, sems.at[0]),
        pltpu.make_async_copy(bias, held_bias, sems.at[1]),
    ])


def assemble(own, other, cache, halo_a, halo_b, held, lt, ht, left, right, kept, stage, wide, sems):
    half = lax.axis_index("tm")
    first, second = 4 * half, 4 - 4 * half
    start, at, edge = 14 * half, 3 - 3 * half, 20 * half
    run_copies([
        pltpu.make_async_copy(
            own, stage.at[pl.ds(first, 4), pl.ds(at, 20)], sems.at[0]),
        pltpu.make_async_copy(
            other.at[:, pl.ds(start, 20)], stage.at[pl.ds(second, 4), pl.ds(at, 20)], sems.at[1]),
        pltpu.make_async_copy(
            cache, stage.at[8:14, pl.ds(at, 20)], sems.at[2]),
        pltpu.make_async_copy(
            halo_a.at[0:4], stage.at[pl.ds(first, 4), pl.ds(edge, 3)], sems.at[3]),
        pltpu.make_async_copy(halo_a.at[4:10], stage.at[8:14, pl.ds(edge, 3)], sems.at[4]),
        pltpu.make_async_copy(
            halo_b, stage.at[pl.ds(second, 4), pl.ds(edge, 3)], sems.at[5]),
    ])
    sub = lax.broadcasted_iota(jnp.int32, (T, C), 0)
    for slot in range(4):
        wide[slot, 14 * COLS:16 * COLS] = jnp.zeros((2 * COLS, 128), F32)

    def row(e, slot):
        for frame in range(14):
            v = stage[frame, e].astype(F32)
            wide[2 * slot, frame * COLS:(frame + 1) * COLS] = v[:, :128]
            wide[2 * slot + 1, frame * COLS:(frame + 1) * COLS] = v[:, 128:]
        past = []
        for col in range(COLS):
            lat = jnp.concatenate(
                [wide[2 * slot + lane, pl.ds(col, T, stride=COLS)] for lane in (0, 1)], 1)
            old = jnp.concatenate(
                [wide[2 * slot + lane, pl.ds(T * COLS + col, T, stride=COLS)]
                 for lane in (0, 1)], 1)
            lt[e, col] = lat.astype(BF)
            ht[e, col] = old.astype(BF)
            past.append(old)
            if col < 3:
                left[e, col] = lat.astype(BF)
            if col >= 5:
                right[e, col - 5] = lat.astype(BF)
        left[e, 3] = jnp.where(sub < 6, past[0], pltpu.roll(past[2], 6, 0)).astype(BF)
        left[e, 4] = past[1].astype(BF)
        right[e, 3] = jnp.where(sub < 6, past[7], pltpu.roll(past[5], 6, 0)).astype(BF)
        right[e, 4] = past[6].astype(BF)

    def pair(i, carry):
        row(2 * i, 0)
        row(2 * i + 1, 1)
        return carry

    lax.fori_loop(0, EXT // 2, pair, 0)
    row(EXT - 1, 0)


def put(dst, r, at, now, past, layer):
    n = now.shape[0]
    sub = lax.broadcasted_iota(jnp.int32, (n, T, C), 1)

    def roll(v, k):
        k %= T
        return v if k == 0 else pltpu.roll(v, k, 1)

    dst[2, r, at:at + n] = now
    dst[1, r, at:at + n] = jnp.where(sub < 1, roll(past, -2 * layer - 1), roll(now, 1))
    dst[0, r, at:at + n] = jnp.where(sub < 2, roll(past, -2 * layer), roll(now, 2))


def conv(src, rows, groups, held, layer, bias, dst):
    count = sum(n for _, n in groups)
    step = (rows + 1) // 2

    def body(i, carry):
        r = i * (rows - step)
        total = None
        for a in range(3):
            for b in range(3):
                parts = []
                for c in range(3):
                    cols = [src[a, pl.ds(r + b, step), first + c:first + c + n]
                            for first, n in groups]
                    block = cols[0] if len(cols) == 1 else jnp.concatenate(cols, 1)
                    parts.append(block.reshape(step * count * T, C).astype(BF))
                k = layer * LAYER_K + (a * 3 + b) * 3 * C
                part = jnp.dot(
                    jnp.concatenate(parts, 1), held[k:k + 3 * C], preferred_element_type=F32)
                total = part if total is None else total + part
        dst[pl.ds(r, step), 0:count] = (total + bias).reshape(step, count, T, C)
        return carry

    lax.fori_loop(0, 2, body, 0)


def silu(v):
    return v / (1.0 + jnp.exp(-v))


def row_limits(border):
    half, place = lax.axis_index("tm"), lax.axis_index("row")
    low = jnp.where((half == 0) & (place == 0), border, 0)
    high = jnp.where(
        (half == 1) & (place == lax.axis_size("row") - 1), HALF + border, HALF + 2 * border)
    return low, high


def attend_all(hidden, cols, rows, wq, wk, wv, wo, keys, values, qs, ks, vs, mix):
    n = len(cols)
    mean = jnp.mean(hidden * hidden, -1, keepdims=True)
    normed = (hidden * lax.rsqrt(mean + 1e-6)).astype(BF)
    for w, dst in ((wq, qs), (wk, ks), (wv, vs)):
        v = jnp.dot(normed, w[...], preferred_element_type=F32).astype(BF).astype(F32)
        dst[0:HALF] = v.reshape(HALF, n, T, C)
        dst[HALF:] = jnp.zeros((1, n, T, C), F32)
    block = (lax.broadcasted_iota(jnp.int32, (C, C), 0) // HD
             == lax.broadcasted_iota(jnp.int32, (C, C), 1) // HD)
    ones = jnp.where(block, 1.0, 0.0).astype(BF)
    m = rows * n
    t = lax.broadcasted_iota(jnp.int32, (m, T, C), 1)

    def attend(i, carry):
        r = rows * i
        q = qs[pl.ds(r, rows)].reshape(m, T, C) * HD ** -0.5
        k = ks[pl.ds(r, rows)].reshape(m, T, C)
        v = vs[pl.ds(r, rows)].reshape(m, T, C)

        def spread(ref, f):
            return jnp.concatenate(
                [jnp.broadcast_to(ref[f, r + j, c:c + 1], (T, C))[None]
                 for j in range(rows) for c in cols], 0)

        products = [q * spread(keys, f) for f in range(2)]
        for d in range(T):
            products.append(q * (k if d == 0 else pltpu.roll(k, d, 1)))
        flat = jnp.concatenate([p.reshape(m * T, C).astype(BF) for p in products], 0)
        sums = jnp.dot(flat, ones, preferred_element_type=F32).reshape(10, m, T, C)
        scores = [sums[0], sums[1], sums[2]]
        for d in range(1, T):
            seen = t >= d
            if d == T - 1:
                seen = seen | (t % 2 == 0)
            scores.append(jnp.where(seen, sums[2 + d], -1e30))
        peak = functools.reduce(jnp.maximum, scores)
        weights = [jnp.exp(s - peak) for s in scores]
        norm = functools.reduce(jnp.add, weights)
        acc = weights[2] * v
        for f in range(2):
            acc = acc + weights[f] * spread(values, f)
        for d in range(1, T):
            acc = acc + weights[2 + d] * pltpu.roll(v, d, 1)
        mix[pl.ds(r, rows)] = (acc / norm).reshape(rows, n, T, C)
        return carry

    lax.fori_loop(0, (HALF + 1) // rows, attend, 0)
    mixed = mix[0:HALF].reshape(HALF * n * T, C).astype(BF)
    return hidden + jnp.dot(mixed, wo[...], preferred_element_type=F32)


def interior(lt, ht, held, bias, wq, wk, wv, wo, key_cache, value_cache, out, kept, x, y, z,
             keys, values, res, qs, ks, vs, mix, ck, cv, sems):
    del kept
    half = lax.axis_index("tm")
    copies = [
        pltpu.make_async_copy(key_cache.at[:, pl.ds(HALF * half, HALF)], ck, sems.at[0]),
        pltpu.make_async_copy(value_cache.at[:, pl.ds(HALF * half, HALF)], cv, sems.at[1]),
    ]
    for copy in copies:
        copy.start()

    def fill(r, carry):
        put(x, r, 3, lt[r].astype(F32), ht[r].astype(F32), 0)
        return carry

    lax.fori_loop(0, EXT, fill, 0)
    conv(x, 21, [(3, 6)], held, 0, bias[0:1], res)
    low, high = row_limits(2)

    def one(r, carry):
        v = jnp.where((r >= low) & (r < high), silu(res[r]), 0.0).astype(BF)
        put(y, r, 3, v.astype(F32), ht[r + 1, 1:7].astype(F32), 1)
        return carry

    lax.fori_loop(0, 21, one, 0)
    conv(y, 19, [(3, 4)], held, 1, bias[1:2], res)
    low2, high2 = row_limits(1)

    def two(r, carry):
        v = jnp.where((r >= low2) & (r < high2), silu(res[r, 0:4]), 0.0).astype(BF)
        put(z, r, 3, v.astype(F32), ht[r + 2, 2:6].astype(F32), 2)
        return carry

    lax.fori_loop(0, 19, two, 0)
    conv(z, 17, [(3, 2)], held, 2, bias[2:3], res)
    hidden = (res[0:17, 0:2] + lt[3:20, 3:5].astype(F32)).astype(BF).astype(F32)
    for copy in copies:
        copy.wait()
    for src, dst in ((ck, keys), (cv, values)):
        dst[:, 0:HALF] = src[...].astype(F32)
        dst[:, HALF:] = jnp.zeros((2, 1, COLS, C), F32)
    done = attend_all(hidden.reshape(HALF * 2 * T, C), (3, 4), 9, wq, wk, wv, wo, keys, values,
                      qs, ks, vs, mix)
    out[...] = done.reshape(HALF, 2, T, C).astype(BF)


def exterior(lt, ht, from_left, from_right, inner, held, bias, wq, wk, wv, wo, x0, y0, z0,
             keys, values, mine, theirs, x, y, z, res, qs, ks, vs, mix, enc):
    del x0, y0, z0
    half = lax.axis_index("tm")
    place = lax.axis_index("col")
    has_left = place > 0
    has_right = place < lax.axis_size("col") - 1

    def fill(r, carry):
        for side, at in ((from_left, 0), (from_right, 11)):
            t1 = side[r, 3].astype(F32)
            t2 = side[r, 4].astype(F32)
            t3 = pltpu.roll(t1, 2, 0)
            order = (t3, t2, t1) if at == 0 else (t1, t2, t3)
            past = jnp.concatenate([v[None] for v in order], 0)
            put(x, r, at, side[r, 0:3].astype(F32), past, 0)
        return carry

    lax.fori_loop(0, EXT, fill, 0)
    conv(x, 21, [(0, 3), (9, 3)], held, 0, bias[0:1], res)
    low, high = row_limits(2)

    def one(r, carry):
        ok = (r >= low) & (r < high)
        v = silu(res[r]).astype(BF).astype(F32)
        e = r + 1
        put(y, r, 0, jnp.concatenate(
            [jnp.where(ok & has_left, v[0:2], 0.0), jnp.where(ok, v[2:3], 0.0)], 0),
            jnp.concatenate([from_left[e, 4:5].astype(F32), from_left[e, 3:4].astype(F32),
                             ht[e, 0:1].astype(F32)], 0), 1)
        put(y, r, 9, jnp.concatenate(
            [jnp.where(ok, v[3:4], 0.0), jnp.where(ok & has_right, v[4:6], 0.0)], 0),
            jnp.concatenate([ht[e, 7:8].astype(F32), from_right[e, 3:4].astype(F32),
                             from_right[e, 4:5].astype(F32)], 0), 1)
        return carry

    lax.fori_loop(0, 21, one, 0)
    conv(y, 19, [(0, 3), (7, 3)], held, 1, bias[1:2], res)
    low2, high2 = row_limits(1)

    def two(r, carry):
        ok = (r >= low2) & (r < high2)
        v = silu(res[r]).astype(BF).astype(F32)
        e = r + 2
        put(z, r, 0, jnp.concatenate(
            [jnp.where(ok & has_left, v[0:1], 0.0), jnp.where(ok, v[1:3], 0.0)], 0),
            jnp.concatenate([from_left[e, 3:4].astype(F32), ht[e, 0:2].astype(F32)], 0), 2)
        put(z, r, 7, jnp.concatenate(
            [jnp.where(ok, v[3:5], 0.0), jnp.where(ok & has_right, v[5:6], 0.0)], 0),
            jnp.concatenate([ht[e, 6:8].astype(F32), from_right[e, 3:4].astype(F32)], 0), 2)
        return carry

    lax.fori_loop(0, 19, two, 0)
    conv(z, 17, [(0, 3), (5, 3)], held, 2, bias[2:3], res)
    cols = (0, 1, 2, 5, 6, 7)
    own = jnp.concatenate([lt[3:20, 0:3], lt[3:20, 5:8]], 1).astype(F32)
    hidden = (res[0:17] + own).astype(BF).astype(F32)
    done = attend_all(hidden.reshape(HALF * 6 * T, C), cols, 3, wq, wk, wv, wo, keys, values,
                      qs, ks, vs, mix).reshape(HALF, 6, T, C)
    done = jnp.concatenate([done[:, 0:3], inner[...].astype(F32), done[:, 3:6]], 1)
    done = done.reshape(HALF * COLS * T, C)
    enc[0] = done[:, :128]
    enc[1] = done[:, 128:]

    def turn(r, carry):
        for dst, base in ((mine, 4 * half), (theirs, 4 - 4 * half)):
            for f in range(4):
                v = jnp.concatenate(
                    [enc[lane, pl.ds(r * COLS * T + base + f, COLS, stride=T)]
                     for lane in (0, 1)], 1)
                dst[f, r] = v.astype(BF)
        return carry

    lax.fori_loop(0, HALF, turn, 0)


def merge(mine, got, out, sems):
    half = lax.axis_index("tm")
    run_copies([
        pltpu.make_async_copy(mine, out.at[:, pl.ds(HALF * half, HALF)], sems.at[0]),
        pltpu.make_async_copy(got, out.at[:, pl.ds(HALF - HALF * half, HALF)], sems.at[1]),
    ])


def local(latent, conv_cache, conv_weight, conv_bias, w_query, w_key, w_value, w_out,
          cache_key, cache_value):
    params = functools.partial(pltpu.CompilerParams)
    cache = conv_cache.reshape(6, ROWS, COLS, C)
    weights = conv_weight.reshape(3 * LAYER_K, C)
    n_row, n_col = lax.axis_size("row"), lax.axis_size("col")

    def device(tm, row):
        return tm * n_row + row

    msg_a, msg_b, own, old = pl.pallas_call(
        pack_rows,
        out_shape=(shape(10, 3, COLS, C), shape(4, 3, COLS, C), shape(4, 20, COLS, C),
                   shape(6, 20, COLS, C)),
        in_specs=[HB, HB],
        out_specs=(VM,) * 4,
        scratch_shapes=[pltpu.SemaphoreType.DMA((5,))],
        compiler_params=params(vmem_limit_bytes=105 << 19),
        name="pack_rows",
    )(latent, cache)
    other = lax.ppermute(latent, "tm", [(0, 1), (1, 0)])
    pairs_a = [(device(0, r), device(0, r + 1)) for r in range(n_row - 1)]
    pairs_a += [(device(1, r + 1), device(1, r)) for r in range(n_row - 1)]
    pairs_b = [(device(1, r), device(0, r + 1)) for r in range(n_row - 1)]
    pairs_b += [(device(0, r + 1), device(1, r)) for r in range(n_row - 1)]
    halo_a = lax.ppermute(msg_a, ("tm", "row"), pairs_a)
    halo_b = lax.ppermute(msg_b, ("tm", "row"), pairs_b)

    held, bias = pl.pallas_call(
        load_weights,
        out_shape=(shape(3 * LAYER_K, C), shape(3, C, dtype=F32)),
        in_specs=[ANY, ANY],
        out_specs=(VM, VM),
        scratch_shapes=[pltpu.SemaphoreType.DMA((2,))],
        cost_estimate=pl.CostEstimate(flops=0, bytes_accessed=11 << 20, transcendentals=0),
        compiler_params=params(vmem_limit_bytes=36 << 20),
        name="load_weights",
    )(weights, conv_bias)

    tiles = shape(EXT, COLS, T, C)
    side = shape(EXT, 5, T, C)
    lt, ht, left, right, held = pl.pallas_call(
        assemble,
        out_shape=(tiles, tiles, side, side, shape(3 * LAYER_K, C)),
        in_specs=[VM] * 6,
        out_specs=(VM,) * 5,
        input_output_aliases={5: 4},
        scratch_shapes=[
            pltpu.VMEM((14, EXT, COLS, C), BF),
            pltpu.VMEM((4, 16 * COLS, 128), F32),
            pltpu.SemaphoreType.DMA((6,)),
        ],
        compiler_params=params(vmem_limit_bytes=18 << 20),
        name="assemble",
    )(own, other, old, halo_a, halo_b, held)
    from_right = lax.ppermute(left, "col", [(i + 1, i) for i in range(n_col - 1)])
    from_left = lax.ppermute(right, "col", [(i, i + 1) for i in range(n_col - 1)])

    grids = (shape(3, 23, 14, T, C, dtype=F32), shape(3, 21, 12, T, C, dtype=F32),
             shape(3, 19, 10, T, C, dtype=F32))
    past = shape(2, HALF + 1, COLS, C, dtype=F32)
    inner, held, x, y, z, keys, values = pl.pallas_call(
        interior,
        out_shape=(shape(17, 2, T, C), shape(3 * LAYER_K, C)) + grids + (past, past),
        in_specs=[VM] * 8 + [ANY] * 2,
        out_specs=(VM,) * 7,
        input_output_aliases={2: 1},
        scratch_shapes=[pltpu.VMEM((21, 6, T, C), F32)]
        + [pltpu.VMEM((HALF + 1, 2, T, C), F32)] * 4
        + [pltpu.VMEM((2, HALF, COLS, C), BF)] * 2
        + [pltpu.SemaphoreType.DMA((2,))],
        cost_estimate=pl.CostEstimate(
            flops=2 * 1888 * LAYER_K * C, bytes_accessed=14 << 20, transcendentals=0),
        compiler_params=params(vmem_limit_bytes=18 << 20),
        name="interior",
    )(lt, ht, held, bias, w_query, w_key, w_value, w_out, cache_key, cache_value)

    mine, theirs, _, _, _ = pl.pallas_call(
        exterior,
        out_shape=(shape(4, HALF, COLS, C), shape(4, HALF, COLS, C)) + grids,
        in_specs=[VM] * 16,
        out_specs=(VM,) * 5,
        input_output_aliases={11: 2, 12: 3, 13: 4},
        scratch_shapes=[pltpu.VMEM((21, 6, T, C), F32)]
        + [pltpu.VMEM((HALF + 1, 6, T, C), F32)] * 4
        + [pltpu.VMEM((2, HALF * COLS * T, 128), F32)],
        cost_estimate=pl.CostEstimate(
            flops=2 * 3000 * LAYER_K * C, bytes_accessed=18 << 20, transcendentals=0),
        compiler_params=params(vmem_limit_bytes=18 << 20),
        name="exterior",
    )(lt, ht, from_left, from_right, inner, held, bias, w_query, w_key, w_value, w_out, x, y, z,
      keys, values)
    got = lax.ppermute(theirs, "tm", [(0, 1), (1, 0)])
    return pl.pallas_call(
        merge,
        out_shape=shape(4, ROWS, COLS, C),
        in_specs=[VM, VM],
        out_specs=HB,
        scratch_shapes=[pltpu.SemaphoreType.DMA((2,))],
        compiler_params=params(vmem_limit_bytes=30 << 20),
        name="merge",
    )(mine, got)


def solution(mesh):
    return jax.shard_map(
        local,
        mesh=mesh,
        in_specs=(
            P("tm", "row", "col", None),
            P(None, None, "row", "col", None),
            P(),
            P(),
            P(),
            P(),
            P(),
            P(),
            P(None, "row", "col", None),
            P(None, "row", "col", None),
        ),
        out_specs=P("tm", "row", "col", None),
        check_vma=False,
    )
```

```python
import functools

import jax
import jax.numpy as jnp
from jax import lax
from jax.experimental import pallas as pl
from jax.experimental.pallas import tpu as pltpu
from jax.sharding import PartitionSpec as P

HEADS = 8
HD = 32
C = 256
T = 8
FRAMES = 4
ROWS = 34
HALF = 17
COLS = 8
EXT = HALF + 6
BF = jnp.bfloat16
F32 = jnp.float32
TAPS = [(a, b, c) for a in range(3) for b in range(3) for c in range(3)]
LAYER_K = 27 * C

ANY = pl.BlockSpec(memory_space=pl.ANY)
HB = pl.BlockSpec(memory_space=pltpu.HBM)
VM = pl.BlockSpec(memory_space=pltpu.VMEM)


def shape(*dims, dtype=BF):
    return jax.ShapeDtypeStruct(dims, dtype)


def run_copies(copies):
    for copy in copies:
        copy.start()
    for copy in copies:
        copy.wait()


def pack_rows(latent, cache, out_a, out_b, own, old, sems):
    half = lax.axis_index("tm")
    row_a, row_b, start = 31 * (1 - half), 31 * half, 14 * half
    run_copies([
        pltpu.make_async_copy(latent.at[:, pl.ds(row_a, 3)], out_a.at[0:4], sems.at[0]),
        pltpu.make_async_copy(cache.at[:, pl.ds(row_a, 3)], out_a.at[4:10], sems.at[1]),
        pltpu.make_async_copy(latent.at[:, pl.ds(row_b, 3)], out_b, sems.at[2]),
        pltpu.make_async_copy(latent.at[:, pl.ds(start, 20)], own, sems.at[3]),
        pltpu.make_async_copy(cache.at[:, pl.ds(start, 20)], old, sems.at[4]),
    ])


def load_first(weights, held, sems):
    run_copies([pltpu.make_async_copy(
        weights.at[0:LAYER_K], held.at[0:LAYER_K], sems.at[0])])


def assemble(own, other, cache, halo_a, halo_b, held, lt, ht, left, right, kept, stage, wide, sems):
    half = lax.axis_index("tm")
    first, second = 4 * half, 4 - 4 * half
    start, at, edge = 14 * half, 3 - 3 * half, 20 * half
    run_copies([
        pltpu.make_async_copy(
            own, stage.at[pl.ds(first, 4), pl.ds(at, 20)], sems.at[0]),
        pltpu.make_async_copy(
            other.at[:, pl.ds(start, 20)], stage.at[pl.ds(second, 4), pl.ds(at, 20)], sems.at[1]),
        pltpu.make_async_copy(
            cache, stage.at[8:14, pl.ds(at, 20)], sems.at[2]),
        pltpu.make_async_copy(
            halo_a.at[0:4], stage.at[pl.ds(first, 4), pl.ds(edge, 3)], sems.at[3]),
        pltpu.make_async_copy(halo_a.at[4:10], stage.at[8:14, pl.ds(edge, 3)], sems.at[4]),
        pltpu.make_async_copy(
            halo_b, stage.at[pl.ds(second, 4), pl.ds(edge, 3)], sems.at[5]),
    ])
    sub = lax.broadcasted_iota(jnp.int32, (T, C), 0)
    for slot in range(4):
        wide[slot, 14 * COLS:16 * COLS] = jnp.zeros((2 * COLS, 128), F32)

    def row(e, slot):
        for frame in range(14):
            v = stage[frame, e].astype(F32)
            wide[2 * slot, frame * COLS:(frame + 1) * COLS] = v[:, :128]
            wide[2 * slot + 1, frame * COLS:(frame + 1) * COLS] = v[:, 128:]
        past = []
        for col in range(COLS):
            lat = jnp.concatenate(
                [wide[2 * slot + lane, pl.ds(col, T, stride=COLS)] for lane in (0, 1)], 1)
            old = jnp.concatenate(
                [wide[2 * slot + lane, pl.ds(T * COLS + col, T, stride=COLS)]
                 for lane in (0, 1)], 1)
            lt[e, col] = lat.astype(BF)
            ht[e, col] = old.astype(BF)
            past.append(old)
            if col < 3:
                left[e, col] = lat.astype(BF)
            if col >= 5:
                right[e, col - 5] = lat.astype(BF)
        left[e, 3] = jnp.where(sub < 6, past[0], pltpu.roll(past[2], 6, 0)).astype(BF)
        left[e, 4] = past[1].astype(BF)
        right[e, 3] = jnp.where(sub < 6, past[7], pltpu.roll(past[5], 6, 0)).astype(BF)
        right[e, 4] = past[6].astype(BF)

    def pair(i, carry):
        row(2 * i, 0)
        row(2 * i + 1, 1)
        return carry

    lax.fori_loop(0, EXT // 2, pair, 0)
    row(EXT - 1, 0)


def put(dst, r, at, now, past, layer):
    n = now.shape[0]
    sub = lax.broadcasted_iota(jnp.int32, (n, T, C), 1)

    def roll(v, k):
        k %= T
        return v if k == 0 else pltpu.roll(v, k, 1)

    tile, odd = r // 2, r % 2
    dst[2, tile, odd, at:at + n] = now
    dst[1, tile, odd, at:at + n] = jnp.where(sub < 1, roll(past, -2 * layer - 1), roll(now, 1))
    dst[0, tile, odd, at:at + n] = jnp.where(sub < 2, roll(past, -2 * layer), roll(now, 2))


def conv(src, tiles, groups, held, layer, bias, dst):
    count = sum(n for _, n in groups)

    def block(a, k, c):
        def rows(shift, odd):
            cols = [src[a, shift:shift + tiles, odd, first + c:first + c + n]
                    for first, n in groups]
            return cols[0] if len(cols) == 1 else jnp.concatenate(cols, 1)

        if k == 0:
            v = rows(0, 0) - rows(1, 0)
        elif k == 1:
            v = rows(0, 1) + rows(1, 0)
        elif k == 2:
            v = rows(1, 0) - rows(0, 1)
        else:
            v = rows(0, 1) - rows(1, 1)
        return v.reshape(tiles * count * T, C).astype(BF)

    def weight(a, k):
        def taps(b):
            at = layer * LAYER_K + (a * 3 + b) * 3 * C
            return held[at:at + 3 * C]

        if k in (0, 3):
            return taps(0 if k == 0 else 2)
        outer = (taps(0).astype(F32) + taps(2).astype(F32)) * 0.5
        inner = taps(1).astype(F32) * 0.5
        return (outer + inner if k == 1 else outer - inner).astype(BF)

    def product(k):
        total = None
        for a in range(3):
            part = jnp.dot(jnp.concatenate([block(a, k, c) for c in range(3)], 1),
                           weight(a, k), preferred_element_type=F32)
            total = part if total is None else total + part
        return total

    middle, other = product(1), product(2)
    even = product(0) + (middle + other) + bias
    dst[0:tiles, 0, 0:count] = even.reshape(tiles, count, T, C)
    odd = (middle - other) - product(3) + bias
    dst[0:tiles, 1, 0:count] = odd.reshape(tiles, count, T, C)


def silu(v):
    return v / (1.0 + jnp.exp(-v))


def row_limits(border):
    half, place = lax.axis_index("tm"), lax.axis_index("row")
    low = jnp.where((half == 0) & (place == 0), border, 0)
    high = jnp.where(
        (half == 1) & (place == lax.axis_size("row") - 1), HALF + border, HALF + 2 * border)
    return low, high


def attend_all(hidden, cols, rows, wq, wk, wv, wo, keys, values, qs, ks, vs, mix):
    n = len(cols)
    mean = jnp.mean(hidden * hidden, -1, keepdims=True)
    normed = (hidden * lax.rsqrt(mean + 1e-6)).astype(BF)
    for w, dst in ((wq, qs), (wk, ks), (wv, vs)):
        v = jnp.dot(normed, w[...], preferred_element_type=F32).astype(BF).astype(F32)
        dst[0:HALF] = v.reshape(HALF, n, T, C)
        dst[HALF:] = jnp.zeros((1, n, T, C), F32)
    block = (lax.broadcasted_iota(jnp.int32, (C, C), 0) // HD
             == lax.broadcasted_iota(jnp.int32, (C, C), 1) // HD)
    ones = jnp.where(block, 1.0, 0.0).astype(BF)
    m = rows * n
    t = lax.broadcasted_iota(jnp.int32, (m, T, C), 1)

    def attend(i, carry):
        r = rows * i
        q = qs[pl.ds(r, rows)].reshape(m, T, C) * HD ** -0.5
        k = ks[pl.ds(r, rows)].reshape(m, T, C)
        v = vs[pl.ds(r, rows)].reshape(m, T, C)

        def spread(ref, f):
            return jnp.concatenate(
                [jnp.broadcast_to(ref[f, r + j, c:c + 1], (T, C))[None]
                 for j in range(rows) for c in cols], 0)

        products = [q * spread(keys, f) for f in range(2)]
        for d in range(T):
            products.append(q * (k if d == 0 else pltpu.roll(k, d, 1)))
        flat = jnp.concatenate([p.reshape(m * T, C).astype(BF) for p in products], 0)
        sums = jnp.dot(flat, ones, preferred_element_type=F32).reshape(10, m, T, C)
        scores = [sums[0], sums[1], sums[2]]
        for d in range(1, T):
            seen = t >= d
            if d == T - 1:
                seen = seen | (t % 2 == 0)
            scores.append(jnp.where(seen, sums[2 + d], -1e30))
        peak = functools.reduce(jnp.maximum, scores)
        weights = [jnp.exp(s - peak) for s in scores]
        norm = functools.reduce(jnp.add, weights)
        acc = weights[2] * v
        for f in range(2):
            acc = acc + weights[f] * spread(values, f)
        for d in range(1, T):
            acc = acc + weights[2 + d] * pltpu.roll(v, d, 1)
        mix[pl.ds(r, rows)] = (acc / norm).reshape(rows, n, T, C)
        return carry

    lax.fori_loop(0, (HALF + 1) // rows, attend, 0)
    mixed = mix[0:HALF].reshape(HALF * n * T, C).astype(BF)
    return hidden + jnp.dot(mixed, wo[...], preferred_element_type=F32)


def interior(lt, ht, first, bias, wq, wk, wv, wo, key_cache, value_cache, weights, out, held, x, y, z,
             keys, values, res, qs, ks, vs, mix, ck, cv, sems):
    del first
    half = lax.axis_index("tm")
    copies = [
        pltpu.make_async_copy(key_cache.at[:, pl.ds(HALF * half, HALF)], ck, sems.at[0]),
        pltpu.make_async_copy(value_cache.at[:, pl.ds(HALF * half, HALF)], cv, sems.at[1]),
        pltpu.make_async_copy(weights.at[LAYER_K:2 * LAYER_K], held.at[LAYER_K:2 * LAYER_K],
                              sems.at[2]),
        pltpu.make_async_copy(weights.at[2 * LAYER_K:3 * LAYER_K],
                              held.at[2 * LAYER_K:3 * LAYER_K], sems.at[3]),
    ]
    for copy in copies:
        copy.start()

    def fill(r, carry):
        put(x, r, 3, lt[r].astype(F32), ht[r].astype(F32), 0)
        return carry

    lax.fori_loop(0, EXT, fill, 0, unroll=2)
    conv(x, 11, [(3, 6)], held, 0, bias[0:1], res)
    low, high = row_limits(2)

    def one(r, carry):
        v = jnp.where((r >= low) & (r < high), silu(res[r // 2, r % 2]), 0.0).astype(BF)
        put(y, r, 3, v.astype(F32), ht[r + 1, 1:7].astype(F32), 1)
        return carry

    lax.fori_loop(0, 21, one, 0, unroll=3)
    copies[2].wait()
    conv(y, 10, [(3, 4)], held, 1, bias[1:2], res)
    low2, high2 = row_limits(1)

    def two(r, carry):
        v = jnp.where((r >= low2) & (r < high2), silu(res[r // 2, r % 2, 0:4]), 0.0).astype(BF)
        put(z, r, 3, v.astype(F32), ht[r + 2, 2:6].astype(F32), 2)
        return carry

    lax.fori_loop(0, 19, two, 0, unroll=2)
    copies[3].wait()
    conv(z, 9, [(3, 2)], held, 2, bias[2:3], res)
    hidden = (res[0:9, :, 0:2].reshape(18, 2, T, C)[0:17] + lt[3:20, 3:5].astype(F32)).astype(BF).astype(F32)
    for copy in copies[0:2]:
        copy.wait()
    for src, dst in ((ck, keys), (cv, values)):
        dst[:, 0:HALF] = src[...].astype(F32)
        dst[:, HALF:] = jnp.zeros((2, 1, COLS, C), F32)
    done = attend_all(hidden.reshape(HALF * 2 * T, C), (3, 4), 9, wq, wk, wv, wo, keys, values,
                      qs, ks, vs, mix)
    out[...] = done.reshape(HALF, 2, T, C).astype(BF)


def exterior(lt, ht, from_left, from_right, inner, held, bias, wq, wk, wv, wo, x0, y0, z0,
             keys, values, mine, theirs, x, y, z, res, qs, ks, vs, mix, enc):
    del x0, y0, z0
    half = lax.axis_index("tm")
    place = lax.axis_index("col")
    has_left = place > 0
    has_right = place < lax.axis_size("col") - 1

    def fill(r, carry):
        for side, at in ((from_left, 0), (from_right, 11)):
            t1 = side[r, 3].astype(F32)
            t2 = side[r, 4].astype(F32)
            t3 = pltpu.roll(t1, 2, 0)
            order = (t3, t2, t1) if at == 0 else (t1, t2, t3)
            past = jnp.concatenate([v[None] for v in order], 0)
            put(x, r, at, side[r, 0:3].astype(F32), past, 0)
        return carry

    lax.fori_loop(0, EXT, fill, 0, unroll=2)
    conv(x, 11, [(0, 3), (9, 3)], held, 0, bias[0:1], res)
    low, high = row_limits(2)

    def one(r, carry):
        ok = (r >= low) & (r < high)
        v = silu(res[r // 2, r % 2]).astype(BF).astype(F32)
        e = r + 1
        put(y, r, 0, jnp.concatenate(
            [jnp.where(ok & has_left, v[0:2], 0.0), jnp.where(ok, v[2:3], 0.0)], 0),
            jnp.concatenate([from_left[e, 4:5].astype(F32), from_left[e, 3:4].astype(F32),
                             ht[e, 0:1].astype(F32)], 0), 1)
        put(y, r, 9, jnp.concatenate(
            [jnp.where(ok, v[3:4], 0.0), jnp.where(ok & has_right, v[4:6], 0.0)], 0),
            jnp.concatenate([ht[e, 7:8].astype(F32), from_right[e, 3:4].astype(F32),
                             from_right[e, 4:5].astype(F32)], 0), 1)
        return carry

    lax.fori_loop(0, 21, one, 0, unroll=3)
    conv(y, 10, [(0, 3), (7, 3)], held, 1, bias[1:2], res)
    low2, high2 = row_limits(1)

    def two(r, carry):
        ok = (r >= low2) & (r < high2)
        v = silu(res[r // 2, r % 2]).astype(BF).astype(F32)
        e = r + 2
        put(z, r, 0, jnp.concatenate(
            [jnp.where(ok & has_left, v[0:1], 0.0), jnp.where(ok, v[1:3], 0.0)], 0),
            jnp.concatenate([from_left[e, 3:4].astype(F32), ht[e, 0:2].astype(F32)], 0), 2)
        put(z, r, 7, jnp.concatenate(
            [jnp.where(ok, v[3:5], 0.0), jnp.where(ok & has_right, v[5:6], 0.0)], 0),
            jnp.concatenate([ht[e, 6:8].astype(F32), from_right[e, 3:4].astype(F32)], 0), 2)
        return carry

    lax.fori_loop(0, 19, two, 0, unroll=2)
    conv(z, 9, [(0, 3), (5, 3)], held, 2, bias[2:3], res)
    cols = (0, 1, 2, 5, 6, 7)
    own = jnp.concatenate([lt[3:20, 0:3], lt[3:20, 5:8]], 1).astype(F32)
    hidden = (res[0:9].reshape(18, 6, T, C)[0:17] + own).astype(BF).astype(F32)
    done = attend_all(hidden.reshape(HALF * 6 * T, C), cols, 3, wq, wk, wv, wo, keys, values,
                      qs, ks, vs, mix).reshape(HALF, 6, T, C)
    done = jnp.concatenate([done[:, 0:3], inner[...].astype(F32), done[:, 3:6]], 1)
    done = done.reshape(HALF * COLS * T, C)
    enc[0] = done[:, :128]
    enc[1] = done[:, 128:]

    def turn(r, carry):
        for dst, base in ((mine, 4 * half), (theirs, 4 - 4 * half)):
            for f in range(4):
                v = jnp.concatenate(
                    [enc[lane, pl.ds(r * COLS * T + base + f, COLS, stride=T)]
                     for lane in (0, 1)], 1)
                dst[f, r] = v.astype(BF)
        return carry

    lax.fori_loop(0, HALF, turn, 0)


def merge(mine, got, out, sems):
    half = lax.axis_index("tm")
    run_copies([
        pltpu.make_async_copy(mine, out.at[:, pl.ds(HALF * half, HALF)], sems.at[0]),
        pltpu.make_async_copy(got, out.at[:, pl.ds(HALF - HALF * half, HALF)], sems.at[1]),
    ])


def local(latent, conv_cache, conv_weight, conv_bias, w_query, w_key, w_value, w_out,
          cache_key, cache_value):
    params = functools.partial(pltpu.CompilerParams)
    cache = conv_cache.reshape(6, ROWS, COLS, C)
    weights = conv_weight.reshape(3 * LAYER_K, C)
    n_row, n_col = lax.axis_size("row"), lax.axis_size("col")

    def device(tm, row):
        return tm * n_row + row

    msg_a, msg_b, own, old = pl.pallas_call(
        pack_rows,
        out_shape=(shape(10, 3, COLS, C), shape(4, 3, COLS, C), shape(4, 20, COLS, C),
                   shape(6, 20, COLS, C)),
        in_specs=[HB, HB],
        out_specs=(VM,) * 4,
        scratch_shapes=[pltpu.SemaphoreType.DMA((5,))],
        compiler_params=params(vmem_limit_bytes=105 << 19),
        name="pack_rows",
    )(latent, cache)
    other = lax.ppermute(latent, "tm", [(0, 1), (1, 0)])
    pairs_a = [(device(0, r), device(0, r + 1)) for r in range(n_row - 1)]
    pairs_a += [(device(1, r + 1), device(1, r)) for r in range(n_row - 1)]
    pairs_b = [(device(1, r), device(0, r + 1)) for r in range(n_row - 1)]
    pairs_b += [(device(0, r + 1), device(1, r)) for r in range(n_row - 1)]
    halo_a = lax.ppermute(msg_a, ("tm", "row"), pairs_a)
    halo_b = lax.ppermute(msg_b, ("tm", "row"), pairs_b)

    held = pl.pallas_call(
        load_first,
        out_shape=shape(3 * LAYER_K, C),
        in_specs=[ANY],
        out_specs=VM,
        scratch_shapes=[pltpu.SemaphoreType.DMA((1,))],
        cost_estimate=pl.CostEstimate(flops=0, bytes_accessed=4 << 20, transcendentals=0),
        compiler_params=params(vmem_limit_bytes=36 << 20),
        name="load_weights",
    )(weights)

    tiles = shape(EXT, COLS, T, C)
    side = shape(EXT, 5, T, C)
    lt, ht, left, right, held = pl.pallas_call(
        assemble,
        out_shape=(tiles, tiles, side, side, shape(3 * LAYER_K, C)),
        in_specs=[VM] * 6,
        out_specs=(VM,) * 5,
        input_output_aliases={5: 4},
        scratch_shapes=[
            pltpu.VMEM((14, EXT, COLS, C), BF),
            pltpu.VMEM((4, 16 * COLS, 128), F32),
            pltpu.SemaphoreType.DMA((6,)),
        ],
        compiler_params=params(vmem_limit_bytes=16 << 20),
        name="assemble",
    )(own, other, old, halo_a, halo_b, held)
    from_right = lax.ppermute(left, "col", [(i + 1, i) for i in range(n_col - 1)])
    from_left = lax.ppermute(right, "col", [(i, i + 1) for i in range(n_col - 1)])

    grids = (shape(3, 12, 2, 14, T, C, dtype=F32), shape(3, 11, 2, 12, T, C, dtype=F32),
             shape(3, 10, 2, 10, T, C, dtype=F32))
    past = shape(2, HALF + 1, COLS, C, dtype=F32)
    inner, held, x, y, z, keys, values = pl.pallas_call(
        interior,
        out_shape=(shape(17, 2, T, C), shape(3 * LAYER_K, C)) + grids + (past, past),
        in_specs=[VM] * 8 + [ANY] * 3,
        out_specs=(VM,) * 7,
        input_output_aliases={2: 1},
        scratch_shapes=[pltpu.VMEM((11, 2, 6, T, C), F32)]
        + [pltpu.VMEM((HALF + 1, 2, T, C), F32)] * 4
        + [pltpu.VMEM((2, HALF, COLS, C), BF)] * 2
        + [pltpu.SemaphoreType.DMA((4,))],
        cost_estimate=pl.CostEstimate(
            flops=2 * 1888 * LAYER_K * C, bytes_accessed=14 << 20, transcendentals=0),
        compiler_params=params(vmem_limit_bytes=16 << 20),
        name="interior",
    )(lt, ht, held, conv_bias, w_query, w_key, w_value, w_out, cache_key, cache_value, weights)

    mine, theirs, _, _, _ = pl.pallas_call(
        exterior,
        out_shape=(shape(4, HALF, COLS, C), shape(4, HALF, COLS, C)) + grids,
        in_specs=[VM] * 16,
        out_specs=(VM,) * 5,
        input_output_aliases={11: 2, 12: 3, 13: 4},
        scratch_shapes=[pltpu.VMEM((11, 2, 6, T, C), F32)]
        + [pltpu.VMEM((HALF + 1, 6, T, C), F32)] * 4
        + [pltpu.VMEM((2, HALF * COLS * T, 128), F32)],
        cost_estimate=pl.CostEstimate(
            flops=2 * 3000 * LAYER_K * C, bytes_accessed=18 << 20, transcendentals=0),
        compiler_params=params(vmem_limit_bytes=16 << 20),
        name="exterior",
    )(lt, ht, from_left, from_right, inner, held, conv_bias, w_query, w_key, w_value, w_out, x, y, z,
      keys, values)
    got = lax.ppermute(theirs, "tm", [(0, 1), (1, 0)])
    return pl.pallas_call(
        merge,
        out_shape=shape(4, ROWS, COLS, C),
        in_specs=[VM, VM],
        out_specs=HB,
        scratch_shapes=[pltpu.SemaphoreType.DMA((2,))],
        compiler_params=params(vmem_limit_bytes=30 << 20),
        name="merge",
    )(mine, got)


def solution(mesh):
    return jax.shard_map(
        local,
        mesh=mesh,
        in_specs=(
            P("tm", "row", "col", None),
            P(None, None, "row", "col", None),
            P(),
            P(),
            P(),
            P(),
            P(),
            P(),
            P(None, "row", "col", None),
            P(None, "row", "col", None),
        ),
        out_specs=P("tm", "row", "col", None),
        check_vma=False,
    )
```

```python
import functools

import jax
import jax.numpy as jnp
from jax import lax
from jax.experimental import pallas as pl
from jax.experimental.pallas import tpu as pltpu
from jax.sharding import PartitionSpec as P

HEADS = 8
HD = 32
C = 256
T = 8
FRAMES = 4
ROWS = 34
HALF = 17
COLS = 8
EXT = HALF + 6
BF = jnp.bfloat16
F32 = jnp.float32
TAPS = [(a, b, c) for a in range(3) for b in range(3) for c in range(3)]
LAYER_K = 27 * C

ANY = pl.BlockSpec(memory_space=pl.ANY)
HB = pl.BlockSpec(memory_space=pltpu.HBM)
VM = pl.BlockSpec(memory_space=pltpu.VMEM)


def shape(*dims, dtype=BF):
    return jax.ShapeDtypeStruct(dims, dtype)


def run_copies(copies):
    for copy in copies:
        copy.start()
    for copy in copies:
        copy.wait()


def pack_rows(latent, cache, out_a, out_b, own, old, sems):
    half = lax.axis_index("tm")
    row_a, row_b, start = 31 * (1 - half), 31 * half, 14 * half
    run_copies([
        pltpu.make_async_copy(latent.at[:, pl.ds(row_a, 3)], out_a.at[0:4], sems.at[0]),
        pltpu.make_async_copy(cache.at[:, pl.ds(row_a, 3)], out_a.at[4:10], sems.at[1]),
        pltpu.make_async_copy(latent.at[:, pl.ds(row_b, 3)], out_b, sems.at[2]),
        pltpu.make_async_copy(latent.at[:, pl.ds(start, 20)], own, sems.at[3]),
        pltpu.make_async_copy(cache.at[:, pl.ds(start, 20)], old, sems.at[4]),
    ])


def load_first(weights, held, sems):
    run_copies([pltpu.make_async_copy(
        weights.at[0:LAYER_K], held.at[0:LAYER_K], sems.at[0])])


def assemble(own, other, cache, halo_a, halo_b, held, lt, ht, left, right, kept, stage, wide, sems):
    half = lax.axis_index("tm")
    first, second = 4 * half, 4 - 4 * half
    start, at, edge = 14 * half, 3 - 3 * half, 20 * half
    run_copies([
        pltpu.make_async_copy(
            own, stage.at[pl.ds(first, 4), pl.ds(at, 20)], sems.at[0]),
        pltpu.make_async_copy(
            other.at[:, pl.ds(start, 20)], stage.at[pl.ds(second, 4), pl.ds(at, 20)], sems.at[1]),
        pltpu.make_async_copy(
            cache, stage.at[8:14, pl.ds(at, 20)], sems.at[2]),
        pltpu.make_async_copy(
            halo_a.at[0:4], stage.at[pl.ds(first, 4), pl.ds(edge, 3)], sems.at[3]),
        pltpu.make_async_copy(halo_a.at[4:10], stage.at[8:14, pl.ds(edge, 3)], sems.at[4]),
        pltpu.make_async_copy(
            halo_b, stage.at[pl.ds(second, 4), pl.ds(edge, 3)], sems.at[5]),
    ])
    sub = lax.broadcasted_iota(jnp.int32, (T, C), 0)
    for slot in range(4):
        wide[slot, 14 * COLS:16 * COLS] = jnp.zeros((2 * COLS, 128), F32)

    def row(e, slot):
        for frame in range(14):
            v = stage[frame, e].astype(F32)
            wide[2 * slot, frame * COLS:(frame + 1) * COLS] = v[:, :128]
            wide[2 * slot + 1, frame * COLS:(frame + 1) * COLS] = v[:, 128:]
        past = []
        for col in range(COLS):
            lat = jnp.concatenate(
                [wide[2 * slot + lane, pl.ds(col, T, stride=COLS)] for lane in (0, 1)], 1)
            old = jnp.concatenate(
                [wide[2 * slot + lane, pl.ds(T * COLS + col, T, stride=COLS)]
                 for lane in (0, 1)], 1)
            lt[e, col] = lat.astype(BF)
            ht[e, col] = old.astype(BF)
            past.append(old)
            if col < 3:
                left[e * 4 + col] = lat.astype(BF)
            if col >= 5:
                right[e * 4 + col - 5] = lat.astype(BF)
        left[e * 4 + 3] = jnp.where(sub < 6, past[0], pltpu.roll(past[2], 6, 0)).astype(BF)
        right[e * 4 + 3] = jnp.where(sub < 6, past[7], pltpu.roll(past[5], 6, 0)).astype(BF)
        return past[1], past[6]

    def pair(i, carry):
        for dst, low, high in zip((left, right), row(2 * i, 0), row(2 * i + 1, 1)):
            dst[EXT * 4 + i] = jnp.where(sub < 4, low, pltpu.roll(high, 4, 0)).astype(BF)
        return carry

    lax.fori_loop(0, EXT // 2, pair, 0)
    for dst, low in zip((left, right), row(EXT - 1, 0)):
        dst[EXT * 4 + EXT // 2] = low.astype(BF)


def put(dst, r, at, now, past, layer):
    n = now.shape[0]
    sub = lax.broadcasted_iota(jnp.int32, (n, T, C), 1)

    def roll(v, k):
        k %= T
        return v if k == 0 else pltpu.roll(v, k, 1)

    tile, odd = r // 2, r % 2
    dst[2, tile, odd, at:at + n] = now
    dst[1, tile, odd, at:at + n] = jnp.where(sub < 1, roll(past, -2 * layer - 1), roll(now, 1))
    dst[0, tile, odd, at:at + n] = jnp.where(sub < 2, roll(past, -2 * layer), roll(now, 2))


def conv(src, tiles, groups, held, layer, bias, dst):
    count = sum(n for _, n in groups)

    def block(a, k, c):
        def rows(shift, odd):
            cols = [src[a, shift:shift + tiles, odd, first + c:first + c + n]
                    for first, n in groups]
            return cols[0] if len(cols) == 1 else jnp.concatenate(cols, 1)

        if k == 0:
            v = rows(0, 0) - rows(1, 0)
        elif k == 1:
            v = rows(0, 1) + rows(1, 0)
        elif k == 2:
            v = rows(1, 0) - rows(0, 1)
        else:
            v = rows(0, 1) - rows(1, 1)
        return v.reshape(tiles * count * T, C).astype(BF)

    def weight(a, k):
        def taps(b):
            at = layer * LAYER_K + (a * 3 + b) * 3 * C
            return held[at:at + 3 * C]

        if k in (0, 3):
            return taps(0 if k == 0 else 2)
        outer = (taps(0).astype(F32) + taps(2).astype(F32)) * 0.5
        inner = taps(1).astype(F32) * 0.5
        return (outer + inner if k == 1 else outer - inner).astype(BF)

    def product(k):
        total = None
        for a in range(3):
            part = jnp.dot(jnp.concatenate([block(a, k, c) for c in range(3)], 1),
                           weight(a, k), preferred_element_type=F32)
            total = part if total is None else total + part
        return total

    middle, other = product(1), product(2)
    even = product(0) + (middle + other) + bias
    dst[0:tiles, 0, 0:count] = even.reshape(tiles, count, T, C)
    odd = (middle - other) - product(3) + bias
    dst[0:tiles, 1, 0:count] = odd.reshape(tiles, count, T, C)


def far_past(side, r):
    v = side[EXT * 4 + r // 2].astype(F32)
    return jnp.where(r % 2 == 0, v, pltpu.roll(v, 4, 0))


def silu(v):
    return 0.5 * v * (1.0 + jnp.tanh(0.5 * v))


def row_limits(border):
    half, place = lax.axis_index("tm"), lax.axis_index("row")
    low = jnp.where((half == 0) & (place == 0), border, 0)
    high = jnp.where(
        (half == 1) & (place == lax.axis_size("row") - 1), HALF + border, HALF + 2 * border)
    return low, high


def attend_all(hidden, cols, rows, wq, wk, wv, wo, keys, values, qs, ks, vs, mix):
    n = len(cols)
    mean = jnp.mean(hidden * hidden, -1, keepdims=True)
    normed = (hidden * lax.rsqrt(mean + 1e-6)).astype(BF)
    for w, dst in ((wq, qs), (wk, ks), (wv, vs)):
        v = jnp.dot(normed, w[...], preferred_element_type=F32).astype(BF).astype(F32)
        dst[0:HALF] = v.reshape(HALF, n, T, C)
        dst[HALF:] = jnp.zeros((1, n, T, C), F32)
    block = (lax.broadcasted_iota(jnp.int32, (C, C), 0) // HD
             == lax.broadcasted_iota(jnp.int32, (C, C), 1) // HD)
    ones = jnp.where(block, 1.0, 0.0).astype(BF)
    m = rows * n
    t = lax.broadcasted_iota(jnp.int32, (m, T, C), 1)

    def attend(i, carry):
        r = rows * i
        q = qs[pl.ds(r, rows)].reshape(m, T, C) * HD ** -0.5
        k = ks[pl.ds(r, rows)].reshape(m, T, C)
        v = vs[pl.ds(r, rows)].reshape(m, T, C)

        def spread(ref, f):
            return jnp.concatenate(
                [jnp.broadcast_to(ref[f, r + j, c:c + 1], (T, C))[None]
                 for j in range(rows) for c in cols], 0)

        products = [q * spread(keys, f) for f in range(2)]
        for d in range(T):
            products.append(q * (k if d == 0 else pltpu.roll(k, d, 1)))
        flat = jnp.concatenate([p.reshape(m * T, C).astype(BF) for p in products], 0)
        sums = jnp.dot(flat, ones, preferred_element_type=F32).reshape(10, m, T, C)
        scores = [sums[0], sums[1], sums[2]]
        for d in range(1, T):
            seen = t >= d
            if d == T - 1:
                seen = seen | (t % 2 == 0)
            scores.append(jnp.where(seen, sums[2 + d], -1e30))
        peak = functools.reduce(jnp.maximum, scores)
        weights = [jnp.exp(s - peak) for s in scores]
        norm = functools.reduce(jnp.add, weights)
        acc = weights[2] * v
        for f in range(2):
            acc = acc + weights[f] * spread(values, f)
        for d in range(1, T):
            acc = acc + weights[2 + d] * pltpu.roll(v, d, 1)
        mix[pl.ds(r, rows)] = (acc / norm).reshape(rows, n, T, C)
        return carry

    lax.fori_loop(0, (HALF + 1) // rows, attend, 0)
    mixed = mix[0:HALF].reshape(HALF * n * T, C).astype(BF)
    return hidden + jnp.dot(mixed, wo[...], preferred_element_type=F32)


def interior(lt, ht, first, bias, wq, wk, wv, wo, key_cache, value_cache, weights, out, held, x, y, z,
             keys, values, res, qs, ks, vs, mix, ck, cv, sems):
    del first
    half = lax.axis_index("tm")
    copies = [
        pltpu.make_async_copy(key_cache.at[:, pl.ds(HALF * half, HALF)], ck, sems.at[0]),
        pltpu.make_async_copy(value_cache.at[:, pl.ds(HALF * half, HALF)], cv, sems.at[1]),
        pltpu.make_async_copy(weights.at[LAYER_K:2 * LAYER_K], held.at[LAYER_K:2 * LAYER_K],
                              sems.at[2]),
        pltpu.make_async_copy(weights.at[2 * LAYER_K:3 * LAYER_K],
                              held.at[2 * LAYER_K:3 * LAYER_K], sems.at[3]),
    ]
    for copy in copies:
        copy.start()

    def fill(r, carry):
        put(x, r, 3, lt[r].astype(F32), ht[r].astype(F32), 0)
        return carry

    lax.fori_loop(0, EXT, fill, 0, unroll=2)
    conv(x, 11, [(3, 6)], held, 0, bias[0:1], res)
    low, high = row_limits(2)

    def one(r, carry):
        v = jnp.where((r >= low) & (r < high), silu(res[r // 2, r % 2]), 0.0).astype(BF)
        put(y, r, 3, v.astype(F32), ht[r + 1, 1:7].astype(F32), 1)
        return carry

    lax.fori_loop(0, 21, one, 0, unroll=3)
    copies[2].wait()
    conv(y, 10, [(3, 4)], held, 1, bias[1:2], res)
    low2, high2 = row_limits(1)

    def two(r, carry):
        v = jnp.where((r >= low2) & (r < high2), silu(res[r // 2, r % 2, 0:4]), 0.0).astype(BF)
        put(z, r, 3, v.astype(F32), ht[r + 2, 2:6].astype(F32), 2)
        return carry

    lax.fori_loop(0, 19, two, 0, unroll=2)
    copies[3].wait()
    conv(z, 9, [(3, 2)], held, 2, bias[2:3], res)
    hidden = (res[0:9, :, 0:2].reshape(18, 2, T, C)[0:17] + lt[3:20, 3:5].astype(F32)).astype(BF).astype(F32)
    for copy in copies[0:2]:
        copy.wait()
    for src, dst in ((ck, keys), (cv, values)):
        dst[:, 0:HALF] = src[...].astype(F32)
        dst[:, HALF:] = jnp.zeros((2, 1, COLS, C), F32)
    done = attend_all(hidden.reshape(HALF * 2 * T, C), (3, 4), 9, wq, wk, wv, wo, keys, values,
                      qs, ks, vs, mix)
    out[...] = done.reshape(HALF, 2, T, C).astype(BF)


def exterior(lt, ht, from_left, from_right, inner, held, bias, wq, wk, wv, wo, x0, y0, z0,
             keys, values, mine, theirs, x, y, z, res, qs, ks, vs, mix, enc):
    del x0, y0, z0
    half = lax.axis_index("tm")
    place = lax.axis_index("col")
    has_left = place > 0
    has_right = place < lax.axis_size("col") - 1

    def fill(r, carry):
        for side, at in ((from_left, 0), (from_right, 11)):
            t1 = side[r * 4 + 3].astype(F32)
            t2 = far_past(side, r)
            t3 = pltpu.roll(t1, 2, 0)
            order = (t3, t2, t1) if at == 0 else (t1, t2, t3)
            past = jnp.concatenate([v[None] for v in order], 0)
            put(x, r, at, side[pl.ds(r * 4, 3)].astype(F32), past, 0)
        return carry

    lax.fori_loop(0, EXT, fill, 0, unroll=2)
    conv(x, 11, [(0, 3), (9, 3)], held, 0, bias[0:1], res)
    low, high = row_limits(2)

    def one(r, carry):
        ok = (r >= low) & (r < high)
        v = silu(res[r // 2, r % 2]).astype(BF).astype(F32)
        e = r + 1
        put(y, r, 0, jnp.concatenate(
            [jnp.where(ok & has_left, v[0:2], 0.0), jnp.where(ok, v[2:3], 0.0)], 0),
            jnp.concatenate([far_past(from_left, e)[None], from_left[e * 4 + 3].astype(F32)[None],
                             ht[e, 0:1].astype(F32)], 0), 1)
        put(y, r, 9, jnp.concatenate(
            [jnp.where(ok, v[3:4], 0.0), jnp.where(ok & has_right, v[4:6], 0.0)], 0),
            jnp.concatenate([ht[e, 7:8].astype(F32), from_right[e * 4 + 3].astype(F32)[None],
                             far_past(from_right, e)[None]], 0), 1)
        return carry

    lax.fori_loop(0, 21, one, 0, unroll=3)
    conv(y, 10, [(0, 3), (7, 3)], held, 1, bias[1:2], res)
    low2, high2 = row_limits(1)

    def two(r, carry):
        ok = (r >= low2) & (r < high2)
        v = silu(res[r // 2, r % 2]).astype(BF).astype(F32)
        e = r + 2
        put(z, r, 0, jnp.concatenate(
            [jnp.where(ok & has_left, v[0:1], 0.0), jnp.where(ok, v[1:3], 0.0)], 0),
            jnp.concatenate([from_left[e * 4 + 3].astype(F32)[None], ht[e, 0:2].astype(F32)], 0), 2)
        put(z, r, 7, jnp.concatenate(
            [jnp.where(ok, v[3:5], 0.0), jnp.where(ok & has_right, v[5:6], 0.0)], 0),
            jnp.concatenate([ht[e, 6:8].astype(F32), from_right[e * 4 + 3].astype(F32)[None]], 0), 2)
        return carry

    lax.fori_loop(0, 19, two, 0, unroll=2)
    conv(z, 9, [(0, 3), (5, 3)], held, 2, bias[2:3], res)
    cols = (0, 1, 2, 5, 6, 7)
    own = jnp.concatenate([lt[3:20, 0:3], lt[3:20, 5:8]], 1).astype(F32)
    hidden = (res[0:9].reshape(18, 6, T, C)[0:17] + own).astype(BF).astype(F32)
    done = attend_all(hidden.reshape(HALF * 6 * T, C), cols, 6, wq, wk, wv, wo, keys, values,
                      qs, ks, vs, mix).reshape(HALF, 6, T, C)
    done = jnp.concatenate([done[:, 0:3], inner[...].astype(F32), done[:, 3:6]], 1)
    done = done.reshape(HALF * COLS * T, C)
    enc[0] = done[:, :128]
    enc[1] = done[:, 128:]

    def turn(r, carry):
        for dst, base in ((mine, 4 * half), (theirs, 4 - 4 * half)):
            for f in range(4):
                v = jnp.concatenate(
                    [enc[lane, pl.ds(r * COLS * T + base + f, COLS, stride=T)]
                     for lane in (0, 1)], 1)
                dst[f, r] = v.astype(BF)
        return carry

    lax.fori_loop(0, HALF, turn, 0, unroll=2)


def merge(mine, got, out, sems):
    half = lax.axis_index("tm")
    run_copies([
        pltpu.make_async_copy(mine, out.at[:, pl.ds(HALF * half, HALF)], sems.at[0]),
        pltpu.make_async_copy(got, out.at[:, pl.ds(HALF - HALF * half, HALF)], sems.at[1]),
    ])


def local(latent, conv_cache, conv_weight, conv_bias, w_query, w_key, w_value, w_out,
          cache_key, cache_value):
    params = functools.partial(pltpu.CompilerParams)
    cache = conv_cache.reshape(6, ROWS, COLS, C)
    weights = conv_weight.reshape(3 * LAYER_K, C)
    n_row, n_col = lax.axis_size("row"), lax.axis_size("col")

    def device(tm, row):
        return tm * n_row + row

    msg_a, msg_b, own, old = pl.pallas_call(
        pack_rows,
        out_shape=(shape(10, 3, COLS, C), shape(4, 3, COLS, C), shape(4, 20, COLS, C),
                   shape(6, 20, COLS, C)),
        in_specs=[HB, HB],
        out_specs=(VM,) * 4,
        scratch_shapes=[pltpu.SemaphoreType.DMA((5,))],
        compiler_params=params(vmem_limit_bytes=105 << 19),
        name="pack_rows",
    )(latent, cache)
    other = lax.ppermute(latent, "tm", [(0, 1), (1, 0)])
    pairs_a = [(device(0, r), device(0, r + 1)) for r in range(n_row - 1)]
    pairs_a += [(device(1, r + 1), device(1, r)) for r in range(n_row - 1)]
    pairs_b = [(device(1, r), device(0, r + 1)) for r in range(n_row - 1)]
    pairs_b += [(device(0, r + 1), device(1, r)) for r in range(n_row - 1)]
    halo_a = lax.ppermute(msg_a, ("tm", "row"), pairs_a)
    halo_b = lax.ppermute(msg_b, ("tm", "row"), pairs_b)

    held = pl.pallas_call(
        load_first,
        out_shape=shape(3 * LAYER_K, C),
        in_specs=[ANY],
        out_specs=VM,
        scratch_shapes=[pltpu.SemaphoreType.DMA((1,))],
        cost_estimate=pl.CostEstimate(flops=0, bytes_accessed=4 << 20, transcendentals=0),
        compiler_params=params(vmem_limit_bytes=36 << 20),
        name="load_weights",
    )(weights)

    tiles = shape(EXT, COLS, T, C)
    side = shape(EXT * 4 + (EXT + 1) // 2, T, C)
    lt, ht, left, right, held = pl.pallas_call(
        assemble,
        out_shape=(tiles, tiles, side, side, shape(3 * LAYER_K, C)),
        in_specs=[VM] * 6,
        out_specs=(VM,) * 5,
        input_output_aliases={5: 4},
        scratch_shapes=[
            pltpu.VMEM((14, EXT, COLS, C), BF),
            pltpu.VMEM((4, 16 * COLS, 128), F32),
            pltpu.SemaphoreType.DMA((6,)),
        ],
        compiler_params=params(vmem_limit_bytes=16 << 20),
        name="assemble",
    )(own, other, old, halo_a, halo_b, held)
    from_right = lax.ppermute(left, "col", [(i + 1, i) for i in range(n_col - 1)])
    from_left = lax.ppermute(right, "col", [(i, i + 1) for i in range(n_col - 1)])

    grids = (shape(3, 12, 2, 14, T, C, dtype=F32), shape(3, 11, 2, 12, T, C, dtype=F32),
             shape(3, 10, 2, 10, T, C, dtype=F32))
    past = shape(2, HALF + 1, COLS, C, dtype=F32)
    inner, held, x, y, z, keys, values = pl.pallas_call(
        interior,
        out_shape=(shape(17, 2, T, C), shape(3 * LAYER_K, C)) + grids + (past, past),
        in_specs=[VM] * 8 + [ANY] * 3,
        out_specs=(VM,) * 7,
        input_output_aliases={2: 1},
        scratch_shapes=[pltpu.VMEM((11, 2, 6, T, C), F32)]
        + [pltpu.VMEM((HALF + 1, 2, T, C), F32)] * 4
        + [pltpu.VMEM((2, HALF, COLS, C), BF)] * 2
        + [pltpu.SemaphoreType.DMA((4,))],
        cost_estimate=pl.CostEstimate(
            flops=2 * 1888 * LAYER_K * C, bytes_accessed=14 << 20, transcendentals=0),
        compiler_params=params(vmem_limit_bytes=16 << 20),
        name="interior",
    )(lt, ht, held, conv_bias, w_query, w_key, w_value, w_out, cache_key, cache_value, weights)

    mine, theirs, _, _, _ = pl.pallas_call(
        exterior,
        out_shape=(shape(4, HALF, COLS, C), shape(4, HALF, COLS, C)) + grids,
        in_specs=[VM] * 16,
        out_specs=(VM,) * 5,
        input_output_aliases={11: 2, 12: 3, 13: 4},
        scratch_shapes=[pltpu.VMEM((11, 2, 6, T, C), F32)]
        + [pltpu.VMEM((HALF + 1, 6, T, C), F32)] * 4
        + [pltpu.VMEM((2, HALF * COLS * T, 128), F32)],
        cost_estimate=pl.CostEstimate(
            flops=2 * 3000 * LAYER_K * C, bytes_accessed=18 << 20, transcendentals=0),
        compiler_params=params(vmem_limit_bytes=16 << 20),
        name="exterior",
    )(lt, ht, from_left, from_right, inner, held, conv_bias, w_query, w_key, w_value, w_out, x, y, z,
      keys, values)
    got = lax.ppermute(theirs, "tm", [(0, 1), (1, 0)])
    return pl.pallas_call(
        merge,
        out_shape=shape(4, ROWS, COLS, C),
        in_specs=[VM, VM],
        out_specs=HB,
        scratch_shapes=[pltpu.SemaphoreType.DMA((2,))],
        compiler_params=params(vmem_limit_bytes=30 << 20),
        name="merge",
    )(mine, got)


def solution(mesh):
    return jax.shard_map(
        local,
        mesh=mesh,
        in_specs=(
            P("tm", "row", "col", None),
            P(None, None, "row", "col", None),
            P(),
            P(),
            P(),
            P(),
            P(),
            P(),
            P(None, "row", "col", None),
            P(None, "row", "col", None),
        ),
        out_specs=P("tm", "row", "col", None),
        check_vma=False,
    )
```

```python
import functools

import jax
import jax.numpy as jnp
from jax import lax
from jax.experimental import pallas as pl
from jax.experimental.pallas import tpu as pltpu
from jax.sharding import PartitionSpec as P

HEADS = 8
HD = 32
C = 256
T = 8
FRAMES = 4
ROWS = 34
HALF = 17
COLS = 8
EXT = HALF + 6
BF = jnp.bfloat16
F32 = jnp.float32
TAPS = [(a, b, c) for a in range(3) for b in range(3) for c in range(3)]
LAYER_K = 27 * C

ANY = pl.BlockSpec(memory_space=pl.ANY)
HB = pl.BlockSpec(memory_space=pltpu.HBM)
VM = pl.BlockSpec(memory_space=pltpu.VMEM)


def shape(*dims, dtype=BF):
    return jax.ShapeDtypeStruct(dims, dtype)


def run_copies(copies):
    for copy in copies:
        copy.start()
    for copy in copies:
        copy.wait()


def pack_rows(latent, cache, out_a, out_b, own, old, sems):
    half = lax.axis_index("tm")
    row_a, row_b, start = 31 * (1 - half), 31 * half, 14 * half
    run_copies([
        pltpu.make_async_copy(latent.at[:, pl.ds(row_a, 3)], out_a.at[0:4], sems.at[0]),
        pltpu.make_async_copy(cache.at[:, pl.ds(row_a, 3)], out_a.at[4:10], sems.at[1]),
        pltpu.make_async_copy(latent.at[:, pl.ds(row_b, 3)], out_b, sems.at[2]),
        pltpu.make_async_copy(latent.at[:, pl.ds(start, 20)], own, sems.at[3]),
        pltpu.make_async_copy(cache.at[:, pl.ds(start, 20)], old, sems.at[4]),
    ])


def load_first(weights, held, sems):
    run_copies([pltpu.make_async_copy(
        weights.at[0:LAYER_K], held.at[0:LAYER_K], sems.at[0])])


def assemble(own, other, cache, halo_a, halo_b, held, lt, ht, left, right, kept, stage, wide, sems):
    half = lax.axis_index("tm")
    first, second = 4 * half, 4 - 4 * half
    start, at, edge = 14 * half, 3 - 3 * half, 20 * half
    run_copies([
        pltpu.make_async_copy(
            own, stage.at[pl.ds(first, 4), pl.ds(at, 20)], sems.at[0]),
        pltpu.make_async_copy(
            other.at[:, pl.ds(start, 20)], stage.at[pl.ds(second, 4), pl.ds(at, 20)], sems.at[1]),
        pltpu.make_async_copy(
            cache, stage.at[8:14, pl.ds(at, 20)], sems.at[2]),
        pltpu.make_async_copy(
            halo_a.at[0:4], stage.at[pl.ds(first, 4), pl.ds(edge, 3)], sems.at[3]),
        pltpu.make_async_copy(halo_a.at[4:10], stage.at[8:14, pl.ds(edge, 3)], sems.at[4]),
        pltpu.make_async_copy(
            halo_b, stage.at[pl.ds(second, 4), pl.ds(edge, 3)], sems.at[5]),
    ])
    sub = lax.broadcasted_iota(jnp.int32, (T, C), 0)
    for slot in range(4):
        wide[slot, 14 * COLS:16 * COLS] = jnp.zeros((2 * COLS, 128), F32)

    def row(e, slot):
        for frame in range(14):
            v = stage[frame, e].astype(F32)
            wide[2 * slot, frame * COLS:(frame + 1) * COLS] = v[:, :128]
            wide[2 * slot + 1, frame * COLS:(frame + 1) * COLS] = v[:, 128:]
        past = []
        for col in range(COLS):
            lat = jnp.concatenate(
                [wide[2 * slot + lane, pl.ds(col, T, stride=COLS)] for lane in (0, 1)], 1)
            old = jnp.concatenate(
                [wide[2 * slot + lane, pl.ds(T * COLS + col, T, stride=COLS)]
                 for lane in (0, 1)], 1)
            lt[e, col] = lat.astype(BF)
            ht[e, col] = old.astype(BF)
            past.append(old)
            if col < 3:
                left[e * 4 + col] = lat.astype(BF)
            if col >= 5:
                right[e * 4 + col - 5] = lat.astype(BF)
        left[e * 4 + 3] = jnp.where(sub < 6, past[0], pltpu.roll(past[2], 6, 0)).astype(BF)
        right[e * 4 + 3] = jnp.where(sub < 6, past[7], pltpu.roll(past[5], 6, 0)).astype(BF)
        return past[1], past[6]

    def pair(i, carry):
        for dst, low, high in zip((left, right), row(2 * i, 0), row(2 * i + 1, 1)):
            dst[EXT * 4 + i] = jnp.where(sub < 4, low, pltpu.roll(high, 4, 0)).astype(BF)
        return carry

    lax.fori_loop(0, EXT // 2, pair, 0)
    for dst, low in zip((left, right), row(EXT - 1, 0)):
        dst[EXT * 4 + EXT // 2] = low.astype(BF)


def put(dst, r, at, now, past, layer):
    n = now.shape[0]
    sub = lax.broadcasted_iota(jnp.int32, (n, T, C), 1)

    def roll(v, k):
        k %= T
        return v if k == 0 else pltpu.roll(v, k, 1)

    tile, odd = r // 2, r % 2
    dst[2, tile, odd, at:at + n] = now
    dst[1, tile, odd, at:at + n] = jnp.where(sub < 1, roll(past, -2 * layer - 1), roll(now, 1))
    dst[0, tile, odd, at:at + n] = jnp.where(sub < 2, roll(past, -2 * layer), roll(now, 2))


def conv(src, tiles, groups, held, layer, bias, dst):
    count = sum(n for _, n in groups)

    def block(a, k, c):
        def rows(shift, odd):
            cols = [src[a, shift:shift + tiles, odd, first + c:first + c + n]
                    for first, n in groups]
            return cols[0] if len(cols) == 1 else jnp.concatenate(cols, 1)

        if k == 0:
            v = rows(0, 0) - rows(1, 0)
        elif k == 1:
            v = rows(0, 1) + rows(1, 0)
        elif k == 2:
            v = rows(1, 0) - rows(0, 1)
        else:
            v = rows(0, 1) - rows(1, 1)
        return v.reshape(tiles * count * T, C).astype(BF)

    def weight(a, k):
        def taps(b):
            at = layer * LAYER_K + (a * 3 + b) * 3 * C
            return held[at:at + 3 * C]

        if k in (0, 3):
            return taps(0 if k == 0 else 2)
        outer = (taps(0).astype(F32) + taps(2).astype(F32)) * 0.5
        inner = taps(1).astype(F32) * 0.5
        return (outer + inner if k == 1 else outer - inner).astype(BF)

    def product(k):
        total = None
        for a in range(3):
            part = jnp.dot(jnp.concatenate([block(a, k, c) for c in range(3)], 1),
                           weight(a, k), preferred_element_type=F32)
            total = part if total is None else total + part
        return total

    middle, other = product(1), product(2)
    even = product(0) + (middle + other) + bias
    dst[0:tiles, 0, 0:count] = even.reshape(tiles, count, T, C)
    odd = (middle - other) - product(3) + bias
    dst[0:tiles, 1, 0:count] = odd.reshape(tiles, count, T, C)


def far_past(side, r):
    v = side[EXT * 4 + r // 2].astype(F32)
    return jnp.where(r % 2 == 0, v, pltpu.roll(v, 4, 0))


def silu(v):
    return 0.5 * v * (1.0 + jnp.tanh(0.5 * v))


def row_limits(border):
    half, place = lax.axis_index("tm"), lax.axis_index("row")
    low = jnp.where((half == 0) & (place == 0), border, 0)
    high = jnp.where(
        (half == 1) & (place == lax.axis_size("row") - 1), HALF + border, HALF + 2 * border)
    return low, high


def attend_all(hidden, cols, rows, wq, wk, wv, wo, keys, values, qs, ks, vs, mix):
    n = len(cols)
    mean = jnp.mean(hidden * hidden, -1, keepdims=True)
    normed = (hidden * lax.rsqrt(mean + 1e-6)).astype(BF)
    for w, dst in ((wq, qs), (wk, ks), (wv, vs)):
        v = jnp.dot(normed, w[...], preferred_element_type=F32).astype(BF).astype(F32)
        dst[0:HALF] = v.reshape(HALF, n, T, C)
        dst[HALF:] = jnp.zeros((1, n, T, C), F32)
    block = (lax.broadcasted_iota(jnp.int32, (C, C), 0) // HD
             == lax.broadcasted_iota(jnp.int32, (C, C), 1) // HD)
    ones = jnp.where(block, 1.0, 0.0).astype(BF)
    m = rows * n
    t = lax.broadcasted_iota(jnp.int32, (m, T, C), 1)

    def attend(i, carry):
        r = rows * i
        q = qs[pl.ds(r, rows)].reshape(m, T, C) * HD ** -0.5
        k = ks[pl.ds(r, rows)].reshape(m, T, C)
        v = vs[pl.ds(r, rows)].reshape(m, T, C)

        def spread(ref, f):
            return jnp.concatenate(
                [jnp.broadcast_to(ref[f, r + j, c:c + 1], (T, C))[None]
                 for j in range(rows) for c in cols], 0)

        products = [q * spread(keys, f) for f in range(2)]
        for d in range(T):
            products.append(q * (k if d == 0 else pltpu.roll(k, d, 1)))
        flat = jnp.concatenate([p.reshape(m * T, C).astype(BF) for p in products], 0)
        sums = jnp.dot(flat, ones, preferred_element_type=F32).reshape(10, m, T, C)
        scores = [sums[0], sums[1], sums[2]]
        for d in range(1, T):
            seen = t >= d
            if d == T - 1:
                seen = seen | (t % 2 == 0)
            scores.append(jnp.where(seen, sums[2 + d], -1e30))
        peak = functools.reduce(jnp.maximum, scores)
        weights = [jnp.exp(s - peak) for s in scores]
        norm = functools.reduce(jnp.add, weights)
        acc = weights[2] * v
        for f in range(2):
            acc = acc + weights[f] * spread(values, f)
        for d in range(1, T):
            acc = acc + weights[2 + d] * pltpu.roll(v, d, 1)
        mix[pl.ds(r, rows)] = (acc / norm).reshape(rows, n, T, C)
        return carry

    lax.fori_loop(0, (HALF + 1) // rows, attend, 0)
    mixed = mix[0:HALF].reshape(HALF * n * T, C).astype(BF)
    return hidden + jnp.dot(mixed, wo[...], preferred_element_type=F32)


def interior(lt, ht, first, bias, wq, wk, wv, wo, key_cache, value_cache, weights, out, held, x, y, z,
             keys, values, res, qs, ks, vs, mix, ck, cv, sems):
    del first
    half = lax.axis_index("tm")
    copies = [
        pltpu.make_async_copy(key_cache.at[:, pl.ds(HALF * half, HALF)], ck, sems.at[0]),
        pltpu.make_async_copy(value_cache.at[:, pl.ds(HALF * half, HALF)], cv, sems.at[1]),
        pltpu.make_async_copy(weights.at[LAYER_K:2 * LAYER_K], held.at[LAYER_K:2 * LAYER_K],
                              sems.at[2]),
        pltpu.make_async_copy(weights.at[2 * LAYER_K:3 * LAYER_K],
                              held.at[2 * LAYER_K:3 * LAYER_K], sems.at[3]),
    ]
    for copy in copies:
        copy.start()

    def fill(r, carry):
        put(x, r, 3, lt[r].astype(F32), ht[r].astype(F32), 0)
        return carry

    lax.fori_loop(0, EXT, fill, 0, unroll=2)
    conv(x, 11, [(3, 6)], held, 0, bias[0:1], res)
    low, high = row_limits(2)

    def one(r, carry):
        v = jnp.where((r >= low) & (r < high), silu(res[r // 2, r % 2]), 0.0).astype(BF)
        put(y, r, 3, v.astype(F32), ht[r + 1, 1:7].astype(F32), 1)
        return carry

    lax.fori_loop(0, 21, one, 0, unroll=3)
    copies[2].wait()
    conv(y, 10, [(3, 4)], held, 1, bias[1:2], res)
    low2, high2 = row_limits(1)

    def two(r, carry):
        v = jnp.where((r >= low2) & (r < high2), silu(res[r // 2, r % 2, 0:4]), 0.0).astype(BF)
        put(z, r, 3, v.astype(F32), ht[r + 2, 2:6].astype(F32), 2)
        return carry

    lax.fori_loop(0, 19, two, 0, unroll=2)
    copies[3].wait()
    conv(z, 9, [(3, 2)], held, 2, bias[2:3], res)
    hidden = (res[0:9, :, 0:2].reshape(18, 2, T, C)[0:17] + lt[3:20, 3:5].astype(F32)).astype(BF).astype(F32)
    for copy in copies[0:2]:
        copy.wait()
    for src, dst in ((ck, keys), (cv, values)):
        dst[:, 0:HALF] = src[...].astype(F32)
        dst[:, HALF:] = jnp.zeros((2, 1, COLS, C), F32)
    done = attend_all(hidden.reshape(HALF * 2 * T, C), (3, 4), 18, wq, wk, wv, wo, keys, values,
                      qs, ks, vs, mix)
    out[...] = done.reshape(HALF, 2, T, C).astype(BF)


def exterior(lt, ht, from_left, from_right, inner, held, bias, wq, wk, wv, wo, x0, y0, z0,
             keys, values, mine, theirs, x, y, z, res, qs, ks, vs, mix, enc):
    del x0, y0, z0
    half = lax.axis_index("tm")
    place = lax.axis_index("col")
    has_left = place > 0
    has_right = place < lax.axis_size("col") - 1

    def fill(r, carry):
        for side, at in ((from_left, 0), (from_right, 11)):
            t1 = side[r * 4 + 3].astype(F32)
            t2 = far_past(side, r)
            t3 = pltpu.roll(t1, 2, 0)
            order = (t3, t2, t1) if at == 0 else (t1, t2, t3)
            past = jnp.concatenate([v[None] for v in order], 0)
            put(x, r, at, side[pl.ds(r * 4, 3)].astype(F32), past, 0)
        return carry

    lax.fori_loop(0, EXT, fill, 0, unroll=2)
    conv(x, 11, [(0, 3), (9, 3)], held, 0, bias[0:1], res)
    low, high = row_limits(2)

    def one(r, carry):
        ok = (r >= low) & (r < high)
        v = silu(res[r // 2, r % 2]).astype(BF).astype(F32)
        e = r + 1
        put(y, r, 0, jnp.concatenate(
            [jnp.where(ok & has_left, v[0:2], 0.0), jnp.where(ok, v[2:3], 0.0)], 0),
            jnp.concatenate([far_past(from_left, e)[None], from_left[e * 4 + 3].astype(F32)[None],
                             ht[e, 0:1].astype(F32)], 0), 1)
        put(y, r, 9, jnp.concatenate(
            [jnp.where(ok, v[3:4], 0.0), jnp.where(ok & has_right, v[4:6], 0.0)], 0),
            jnp.concatenate([ht[e, 7:8].astype(F32), from_right[e * 4 + 3].astype(F32)[None],
                             far_past(from_right, e)[None]], 0), 1)
        return carry

    lax.fori_loop(0, 21, one, 0, unroll=3)
    conv(y, 10, [(0, 3), (7, 3)], held, 1, bias[1:2], res)
    low2, high2 = row_limits(1)

    def two(r, carry):
        ok = (r >= low2) & (r < high2)
        v = silu(res[r // 2, r % 2]).astype(BF).astype(F32)
        e = r + 2
        put(z, r, 0, jnp.concatenate(
            [jnp.where(ok & has_left, v[0:1], 0.0), jnp.where(ok, v[1:3], 0.0)], 0),
            jnp.concatenate([from_left[e * 4 + 3].astype(F32)[None], ht[e, 0:2].astype(F32)], 0), 2)
        put(z, r, 7, jnp.concatenate(
            [jnp.where(ok, v[3:5], 0.0), jnp.where(ok & has_right, v[5:6], 0.0)], 0),
            jnp.concatenate([ht[e, 6:8].astype(F32), from_right[e * 4 + 3].astype(F32)[None]], 0), 2)
        return carry

    lax.fori_loop(0, 19, two, 0, unroll=2)
    conv(z, 9, [(0, 3), (5, 3)], held, 2, bias[2:3], res)
    cols = (0, 1, 2, 5, 6, 7)
    own = jnp.concatenate([lt[3:20, 0:3], lt[3:20, 5:8]], 1).astype(F32)
    hidden = (res[0:9].reshape(18, 6, T, C)[0:17] + own).astype(BF).astype(F32)
    done = attend_all(hidden.reshape(HALF * 6 * T, C), cols, 9, wq, wk, wv, wo, keys, values,
                      qs, ks, vs, mix).reshape(HALF, 6, T, C)
    done = jnp.concatenate([done[:, 0:3], inner[...].astype(F32), done[:, 3:6]], 1)
    done = done.reshape(HALF * COLS * T, C)
    enc[0] = done[:, :128]
    enc[1] = done[:, 128:]

    def turn(r, carry):
        for dst, base in ((mine, 4 * half), (theirs, 4 - 4 * half)):
            for f in range(4):
                v = jnp.concatenate(
                    [enc[lane, pl.ds(r * COLS * T + base + f, COLS, stride=T)]
                     for lane in (0, 1)], 1)
                dst[f, r] = v.astype(BF)
        return carry

    lax.fori_loop(0, HALF, turn, 0, unroll=4)


def merge(mine, got, out, sems):
    half = lax.axis_index("tm")
    run_copies([
        pltpu.make_async_copy(mine, out.at[:, pl.ds(HALF * half, HALF)], sems.at[0]),
        pltpu.make_async_copy(got, out.at[:, pl.ds(HALF - HALF * half, HALF)], sems.at[1]),
    ])


def local(latent, conv_cache, conv_weight, conv_bias, w_query, w_key, w_value, w_out,
          cache_key, cache_value):
    params = functools.partial(pltpu.CompilerParams)
    cache = conv_cache.reshape(6, ROWS, COLS, C)
    weights = conv_weight.reshape(3 * LAYER_K, C)
    n_row, n_col = lax.axis_size("row"), lax.axis_size("col")

    def device(tm, row):
        return tm * n_row + row

    msg_a, msg_b, own, old = pl.pallas_call(
        pack_rows,
        out_shape=(shape(10, 3, COLS, C), shape(4, 3, COLS, C), shape(4, 20, COLS, C),
                   shape(6, 20, COLS, C)),
        in_specs=[HB, HB],
        out_specs=(VM,) * 4,
        scratch_shapes=[pltpu.SemaphoreType.DMA((5,))],
        compiler_params=params(vmem_limit_bytes=105 << 19),
        name="pack_rows",
    )(latent, cache)
    other = lax.ppermute(latent, "tm", [(0, 1), (1, 0)])
    pairs_a = [(device(0, r), device(0, r + 1)) for r in range(n_row - 1)]
    pairs_a += [(device(1, r + 1), device(1, r)) for r in range(n_row - 1)]
    pairs_b = [(device(1, r), device(0, r + 1)) for r in range(n_row - 1)]
    pairs_b += [(device(0, r + 1), device(1, r)) for r in range(n_row - 1)]
    halo_a = lax.ppermute(msg_a, ("tm", "row"), pairs_a)
    halo_b = lax.ppermute(msg_b, ("tm", "row"), pairs_b)

    held = pl.pallas_call(
        load_first,
        out_shape=shape(3 * LAYER_K, C),
        in_specs=[ANY],
        out_specs=VM,
        scratch_shapes=[pltpu.SemaphoreType.DMA((1,))],
        cost_estimate=pl.CostEstimate(flops=0, bytes_accessed=4 << 20, transcendentals=0),
        compiler_params=params(vmem_limit_bytes=36 << 20),
        name="load_weights",
    )(weights)

    tiles = shape(EXT, COLS, T, C)
    side = shape(EXT * 4 + (EXT + 1) // 2, T, C)
    lt, ht, left, right, held = pl.pallas_call(
        assemble,
        out_shape=(tiles, tiles, side, side, shape(3 * LAYER_K, C)),
        in_specs=[VM] * 6,
        out_specs=(VM,) * 5,
        input_output_aliases={5: 4},
        scratch_shapes=[
            pltpu.VMEM((14, EXT, COLS, C), BF),
            pltpu.VMEM((4, 16 * COLS, 128), F32),
            pltpu.SemaphoreType.DMA((6,)),
        ],
        compiler_params=params(vmem_limit_bytes=16 << 20),
        name="assemble",
    )(own, other, old, halo_a, halo_b, held)
    from_right = lax.ppermute(left, "col", [(i + 1, i) for i in range(n_col - 1)])
    from_left = lax.ppermute(right, "col", [(i, i + 1) for i in range(n_col - 1)])

    grids = (shape(3, 12, 2, 14, T, C, dtype=F32), shape(3, 11, 2, 12, T, C, dtype=F32),
             shape(3, 10, 2, 10, T, C, dtype=F32))
    past = shape(2, HALF + 1, COLS, C, dtype=F32)
    inner, held, x, y, z, keys, values = pl.pallas_call(
        interior,
        out_shape=(shape(17, 2, T, C), shape(3 * LAYER_K, C)) + grids + (past, past),
        in_specs=[VM] * 8 + [ANY] * 3,
        out_specs=(VM,) * 7,
        input_output_aliases={2: 1},
        scratch_shapes=[pltpu.VMEM((11, 2, 6, T, C), F32)]
        + [pltpu.VMEM((HALF + 1, 2, T, C), F32)] * 4
        + [pltpu.VMEM((2, HALF, COLS, C), BF)] * 2
        + [pltpu.SemaphoreType.DMA((4,))],
        cost_estimate=pl.CostEstimate(
            flops=2 * 1888 * LAYER_K * C, bytes_accessed=14 << 20, transcendentals=0),
        compiler_params=params(vmem_limit_bytes=16 << 20),
        name="interior",
    )(lt, ht, held, conv_bias, w_query, w_key, w_value, w_out, cache_key, cache_value, weights)

    mine, theirs, _, _, _ = pl.pallas_call(
        exterior,
        out_shape=(shape(4, HALF, COLS, C), shape(4, HALF, COLS, C)) + grids,
        in_specs=[VM] * 16,
        out_specs=(VM,) * 5,
        input_output_aliases={11: 2, 12: 3, 13: 4},
        scratch_shapes=[pltpu.VMEM((11, 2, 6, T, C), F32)]
        + [pltpu.VMEM((HALF + 1, 6, T, C), F32)] * 4
        + [pltpu.VMEM((2, HALF * COLS * T, 128), F32)],
        cost_estimate=pl.CostEstimate(
            flops=2 * 3000 * LAYER_K * C, bytes_accessed=18 << 20, transcendentals=0),
        compiler_params=params(vmem_limit_bytes=16 << 20),
        name="exterior",
    )(lt, ht, from_left, from_right, inner, held, conv_bias, w_query, w_key, w_value, w_out, x, y, z,
      keys, values)
    got = lax.ppermute(theirs, "tm", [(0, 1), (1, 0)])
    return pl.pallas_call(
        merge,
        out_shape=shape(4, ROWS, COLS, C),
        in_specs=[VM, VM],
        out_specs=HB,
        scratch_shapes=[pltpu.SemaphoreType.DMA((2,))],
        compiler_params=params(vmem_limit_bytes=30 << 20),
        name="merge",
    )(mine, got)


def solution(mesh):
    return jax.shard_map(
        local,
        mesh=mesh,
        in_specs=(
            P("tm", "row", "col", None),
            P(None, None, "row", "col", None),
            P(),
            P(),
            P(),
            P(),
            P(),
            P(),
            P(None, "row", "col", None),
            P(None, "row", "col", None),
        ),
        out_specs=P("tm", "row", "col", None),
        check_vma=False,
    )
```
